256 devices in a mesh: freq: 4 (over z_hi, core), space: 64 (over z_lo, y, x).
Axes of the slice: x: 4, y: 4, z: 8 (z_hi: 2, z_lo: 4; z = z_hi * 4 + z_lo), core: 2. Of those that a mesh axis runs over, the one named last changes fastest.
Arguments:
- source_field: bfloat16 [2, 8, 1024, 1024], P(None, 'freq', 'space'), may hold values from -6 to 6
- receiver_field: bfloat16 [2, 8, 1024, 1024], P(None, 'freq', 'space'), may hold values from -6 to 6
- line_inverse: bfloat16 [2, 8, 1024, 1024], P(None, 'freq'), may hold values from -0.125 to 0.125
- lens_delay: float32 [3, 1024, 1024], P(None, 'space'), may hold values from -0.6 to 0.6
- omegas: float32 [8], P('freq'), may hold values from 4 to 40
- image_weights: float32 [8], P('freq'), may hold values from 0.1 to 1
Outputs:
- source_out: bfloat16 [2, 8, 1024, 1024], P(None, 'freq', 'space')
- receiver_out: bfloat16 [2, 8, 1024, 1024], P(None, 'freq', 'space')
- gradient: float32 [3, 1024, 1024], P(None, 'space')
The draws below stay inside these ranges and needn't reach their ends.
All inputs are finite; a program needn't handle non-finite values.
Results may differ from the reference program's by a relative error of at most 0.017.
Values may be sent and summed in bfloat16 or wider, within the bound.
A program may use at most 64 MiB of HBM per device.

```python
import math
import jax
import jax.numpy as jnp
from jax import lax

NL = 1024
DEPTHS = 3
FREQS = 8


def levels(stream_key, dims, split, low, high):
    gain = 1.0
    for axis_at, shards_of in split:
        steps = jax.random.uniform(jax.random.fold_in(jax.random.fold_in(stream_key, 6), axis_at), (shards_of,), jnp.float32, low / len(split), high / len(split))
        gain = gain * jnp.repeat(jnp.exp(steps), dims[axis_at] // shards_of).reshape((-1,) + (1,) * (len(dims) - 1 - axis_at))
    return gain


def normal_values(key, shape, scale, limit, pieces=(), held_as=jnp.bfloat16):
    values = jax.random.normal(key, shape, jnp.float32) * scale
    if len(pieces) > 0:
        values = levels(key, shape, pieces, -0.22, 0.18) * values
    return jnp.clip(values, min=-limit, max=limit).astype(held_as)


def setup_inputs(seed: int = 0) -> dict:
    arg_keys = jax.random.split(jax.random.key(seed), 7)
    return {
        "source_field": normal_values(arg_keys[0], (2, FREQS, NL, NL), 1.0, 6.0, ((1, 4), (2, 64))),
        "receiver_field": normal_values(arg_keys[1], (2, FREQS, NL, NL), 1.0, 6.0, ((1, 4), (2, 64))),
        "line_inverse": normal_values(arg_keys[2], (2, FREQS, NL, NL), (2 * NL) ** -0.5, 0.125, ((1, 4),)),
        "lens_delay": normal_values(arg_keys[3], (DEPTHS, NL, NL), 0.1, 0.6, ((1, 64),), jnp.float32),
        "omegas": jnp.clip(jnp.exp(math.log(40.0) - 2.3025851 * jax.random.uniform(arg_keys[4], (FREQS,), jnp.float32) ** levels(arg_keys[4], (FREQS,), ((0, 4),), -0.2, 0.2)), 4.0, 40.0),
        "image_weights": jnp.clip(jnp.exp(math.log(1.0) - 2.3025851 * jax.random.uniform(arg_keys[5], (FREQS,), jnp.float32) ** levels(arg_keys[5], (FREQS,), ((0, 4),), -0.2, 0.2)), 0.1, 1.0),
    }


def combine_parts(prod_real, prod_imag, flip_sign):
    new_real = prod_real[:, 0] - flip_sign * prod_imag[:, 1]
    new_imag = prod_real[:, 1] + flip_sign * prod_imag[:, 0]
    return jnp.stack([new_real, new_imag], axis=1)


def reference(source_field, receiver_field, line_inverse, lens_delay, omegas, image_weights):
    wavefields = jnp.stack([source_field, receiver_field]).astype(jnp.float32)
    matrix_real = line_inverse[0].astype(jnp.float32)
    matrix_imag = line_inverse[1].astype(jnp.float32)
    flip_sign = jnp.array([1.0, -1.0], jnp.float32).reshape(2, 1, 1, 1)
    slices = []
    for depth_step in range(DEPTHS):
        phase_angle = omegas[:, None, None] * lens_delay[depth_step][None]
        cosine = jnp.cos(phase_angle)
        sine_part = jnp.sin(phase_angle)
        real_part = wavefields[:, 0]
        imag_part = wavefields[:, 1]
        phased = jnp.stack([real_part * cosine + flip_sign * imag_part * sine_part,
                            imag_part * cosine - flip_sign * real_part * sine_part], axis=1).astype(jnp.bfloat16)
        phased_wide = phased.astype(jnp.float32)
        prod_real = jnp.einsum("fij,wpfyj->wpfyi", matrix_real, phased_wide, precision=lax.Precision.HIGHEST)
        prod_imag = jnp.einsum("fij,wpfyj->wpfyi", matrix_imag, phased_wide, precision=lax.Precision.HIGHEST)
        across = combine_parts(prod_real, prod_imag, flip_sign).astype(jnp.bfloat16).astype(jnp.float32)
        prod_real = jnp.einsum("fij,wpfjx->wpfix", matrix_real, across, precision=lax.Precision.HIGHEST)
        prod_imag = jnp.einsum("fij,wpfjx->wpfix", matrix_imag, across, precision=lax.Precision.HIGHEST)
        wavefields = combine_parts(prod_real, prod_imag, flip_sign)
        image_term = wavefields[0, 0] * wavefields[1, 0] + wavefields[0, 1] * wavefields[1, 1]
        slices.append(jnp.sum(image_weights[:, None, None] * image_term, axis=0))
    return (wavefields[0].astype(jnp.bfloat16), wavefields[1].astype(jnp.bfloat16), jnp.stack(slices))
```

```python
import jax
import jax.numpy as jnp
from jax import lax
from jax.experimental import pallas as pl
from jax.experimental.pallas import tpu as pltpu
from jax.sharding import PartitionSpec as P

F32 = jnp.float32
BF16 = jnp.bfloat16
MESH = pl.DeviceIdType.MESH
LANES = 128
BLOCK = 32
NL = 1024
ROWS = 16
GROUP = 32
SHARDS = 64
CHUNK = 256
NT = (((1,), (1,)), ((), ()))
SWAP_SIGN = (-1.0, 1.0, 1.0, -1.0)

(A2A1, A2A2, A2A3, A2A4, LENS1, LENS2, FWD1, FWD2,
 SUM0, DIST0, SUM1, DIST1, PAIR, CROSS) = range(14)
PHASES = 14


def lanes(tile):
    return lax.broadcasted_iota(jnp.int32, tile.shape, 1)


def turn(tile, shift):
    return pltpu.roll(tile, shift % LANES, 1)


def even_block(tile):
    return (lanes(tile) // BLOCK) % 2 == 0


def block_transpose(tiles):
    t0, t1, t2, t3 = tiles
    low = lanes(t0) < 64
    even = even_block(t0)
    a0, a2 = jnp.where(low, t0, turn(t2, 64)), jnp.where(low, turn(t0, 64), t2)
    a1, a3 = jnp.where(low, t1, turn(t3, 64)), jnp.where(low, turn(t1, 64), t3)
    b0, b1 = jnp.where(even, a0, turn(a1, 32)), jnp.where(even, turn(a0, -32), a1)
    b2, b3 = jnp.where(even, a2, turn(a3, 32)), jnp.where(even, turn(a2, -32), a3)
    return b0, b1, b2, b3


def swap_parts(tile):
    return jnp.where(even_block(tile), turn(tile, -32), turn(tile, 32))


def outer_sign(tile):
    block = lanes(tile) // BLOCK
    return jnp.where((block == 0) | (block == 3), -1.0, 1.0)


def cos_sin(theta):
    n = jnp.floor(theta * 0.3183098861837907 + 0.5)
    r = theta - n * 3.140625
    r = r - n * 9.67502593994140625e-4
    r = r - n * 1.509957990978376e-7
    flip = 1.0 - 2.0 * (n - 2.0 * jnp.floor(n * 0.5))
    z = r * r
    s = -1.0 / 39916800.0
    for term in (1.0 / 362880.0, -1.0 / 5040.0, 1.0 / 120.0, -1.0 / 6.0, 1.0):
        s = s * z + term
    c = 1.0 / 479001600.0
    for term in (-1.0 / 3628800.0, 1.0 / 40320.0, -1.0 / 720.0, 1.0 / 24.0, -0.5, 1.0):
        c = c * z + term
    return c * flip, s * r * flip


def at(index, size):
    return pl.ds(pl.multiple_of(index * size, size), size)


def kernel(src, rcv, minv, lens, om, wt, src_out, rcv_out, grad,
           src_v, rcv_v, lens_v, m, send1, got1, send2, got2, send3, got3, send4, got4,
           ya, yb, xa, xb, xf, cos1, sin1, cos2, sin2, lens1, lens2_send, lens2,
           part0, sum0, dist0_send, dist0, part1, sum1, dist1_send, dist1,
           pair, cross, load_sem, ss, rs):
    fq = lax.axis_index("freq")
    s = lax.axis_index("space")
    h = s // GROUP
    k = lax.rem(s, GROUP)
    core = lax.rem(fq, 2)
    z_hi = fq // 2
    rank = 2 * fq + h
    mine = lax.rem(s, 2) == core
    om_h = om[h]
    wt_h = wt[h]

    def remote(source, target, phase, freq, space):
        return pltpu.make_async_remote_copy(
            src_ref=source, dst_ref=target, send_sem=ss.at[phase], recv_sem=rs.at[phase],
            device_id={"freq": freq, "space": space}, device_id_type=MESH)

    def wait_on(sem, ref):
        pltpu.make_async_copy(ref, ref, sem).wait()

    def give(source, target, phase, freq, space):
        here = (freq == fq) & (space == s)

        @pl.when(here)
        def _():
            pltpu.make_async_copy(source, target, rs.at[phase]).start()

        @pl.when(jnp.logical_not(here))
        def _():
            remote(source, target, phase, freq, space).start()

    loads = [
        pltpu.make_async_copy(src, src_v, load_sem.at[0]),
        pltpu.make_async_copy(rcv, rcv_v, load_sem.at[1]),
        pltpu.make_async_copy(lens, lens_v, load_sem.at[2]),
        pltpu.make_async_copy(minv.at[:, h], m.at[0], load_sem.at[3]),
        pltpu.make_async_copy(minv.at[:, 1 - h], m.at[1], load_sem.at[4]),
    ]
    for load in loads:
        load.start()
    barrier = pltpu.get_barrier_semaphore()

    def greet(i, carry):
        pl.semaphore_signal(barrier, inc=1, device_id={"freq": fq, "space": lax.rem(s + i, SHARDS)},
                            device_id_type=MESH)
        return carry

    lax.fori_loop(1, SHARDS, greet, 0)
    for i in range(1, 4):
        pl.semaphore_signal(barrier, inc=1, device_id={"freq": lax.rem(fq + i, 4), "space": s},
                            device_id_type=MESH)
    for load in loads[:3]:
        load.wait()

    def rotate0(i, carry):
        f = i // 8
        q = lax.rem(i, 8)
        c, sn = cos_sin(om[f] * lens_v[0, :, at(q, LANES)])
        sre = src_v[0, f, :, at(q, LANES)].astype(F32)
        sim = src_v[1, f, :, at(q, LANES)].astype(F32)
        rre = rcv_v[0, f, :, at(q, LANES)].astype(F32)
        rim = rcv_v[1, f, :, at(q, LANES)].astype(F32)
        tiles = block_transpose((sre * c + sim * sn, sim * c - sre * sn,
                                 rre * c - rim * sn, rim * c + rre * sn))
        for p in range(4):
            send1[at(f * GROUP + 4 * q + p, ROWS), :] = tiles[p].astype(BF16)
        return carry

    lax.fori_loop(0, 16, rotate0, 0)
    got1[at(s, ROWS), :] = send1[at(s, ROWS), :]
    pl.semaphore_wait(barrier, SHARDS - 1 + 3)

    def go1(i, carry):
        t = lax.rem(s + i, SHARDS)
        remote(send1.at[at(t, ROWS)], got1.at[at(s, ROWS)], A2A1, fq, t).start()
        return carry

    lax.fori_loop(1, SHARDS, go1, 0)

    @pl.when(mine)
    def _():
        for half in range(2):
            give(lens_v.at[1], lens1.at[core], LENS1, fq, half * GROUP + s // 2)

    def pack2(q, carry):
        value = lens_v[2, :, at(q, LANES)]
        high = value.astype(BF16).astype(F32)
        rest = value - high
        middle = rest.astype(BF16).astype(F32)
        tiles = block_transpose((high, middle, rest - middle, jnp.zeros_like(value)))
        for p in range(4):
            lens2_send[at(4 * q + p, ROWS), :] = tiles[p].astype(BF16)
        return carry

    lax.fori_loop(0, 8, pack2, 0)

    def y_operands(got, other):
        def body(i, carry):
            tile = got[at(i, 128), :].astype(F32)
            other[at(i, 128), :] = (swap_parts(tile) * outer_sign(tile)).astype(BF16)
            return carry

        lax.fori_loop(0, 8, body, 0)

    def y_solve(first, second, n):
        rows = at(n, CHUNK)
        return (jnp.dot(m[0, 0, rows, :], first[...], preferred_element_type=F32)
                + jnp.dot(m[0, 1, rows, :], second[...], preferred_element_type=F32))

    def x_solve(f, first, second, n):
        rows = at(n, CHUNK)
        return (lax.dot_general(first, m[f, 0, rows, :], NT, preferred_element_type=F32)
                + lax.dot_general(second, m[f, 1, rows, :], NT, preferred_element_type=F32))

    def send_group(send, got, phase, n):
        def body(i, carry):
            t = n * 8 + lax.rem(k + i, 8)

            @pl.when(t != k)
            def _():
                remote(send.at[at(t, BLOCK)], got.at[at(k, BLOCK)], phase, fq, h * GROUP + t).start()

            return carry

        lax.fori_loop(0, 8, body, 0)

    loads[3].wait()
    wait_on(rs.at[A2A1], got1.at[pl.ds(0, ROWS * (SHARDS - 1))])
    y_operands(got1, ya)

    def solve1(i, carry):
        n = lax.rem(k // 8 + i, 4)
        send2[at(n, CHUNK), :] = y_solve(got1, ya, n).astype(BF16)
        send_group(send2, got2, A2A2, n)
        return carry

    lax.fori_loop(0, 4, solve1, 0)
    got2[at(k, BLOCK), :] = send2[at(k, BLOCK), :]

    wait_on(rs.at[LENS1], lens1.at[0])
    forward1 = remote(lens1.at[core], lens1.at[core], FWD1, fq + 1 - 2 * core, s)
    forward1.start()

    skew = jnp.where(mine, 0, 1)

    def go_lens2(i, carry):
        t = lax.rem(s + skew + 2 * i, SHARDS)

        @pl.when(t != s)
        def _():
            remote(lens2_send.at[at(lax.rem(t, GROUP), ROWS)], lens2.at[at(s, ROWS)], LENS2, fq, t).start()

        return carry

    lax.fori_loop(0, 32, go_lens2, 0)

    @pl.when(mine)
    def _():
        lens2[at(s, ROWS), :] = lens2_send[at(k, ROWS), :]

    forward1.wait_recv()

    def trig1(q, carry):
        for b in range(2):
            c, sn = cos_sin(om_h * lens1[b, :, at(q, LANES)])
            cos1[pl.ds(b * ROWS, ROWS), at(q, LANES)] = c
            sin1[pl.ds(b * ROWS, ROWS), at(q, LANES)] = sn
        return carry

    lax.fori_loop(0, 8, trig1, 0)

    wait_on(rs.at[A2A2], got2.at[pl.ds(0, BLOCK * (GROUP - 1))])

    def gather2(q, carry):
        tiles = block_transpose([got2[at(4 * q + p, BLOCK), :].astype(F32) for p in range(4)])
        for c in range(4):
            xa[0, pl.ds(c * BLOCK, BLOCK), at(q, LANES)] = tiles[c].astype(BF16)
            xa[1, pl.ds(c * BLOCK, BLOCK), at(q, LANES)] = (SWAP_SIGN[c] * tiles[c ^ 1]).astype(BF16)
        return carry

    lax.fori_loop(0, 8, gather2, 0)

    def solve2(n, carry):
        new = x_solve(0, xa[0], xa[1], n)
        sre, sim, rre, rim = (new[c * BLOCK:(c + 1) * BLOCK] for c in range(4))
        image = wt_h * (sre * rre + sim * rim)
        for u in range(2):
            part0[2 * n + u] = image[:, u * LANES:(u + 1) * LANES].astype(BF16)
        c, sn = cos1[:, at(n, CHUNK)], sin1[:, at(n, CHUNK)]
        turned = (sre * c + sim * sn, sim * c - sre * sn, rre * c - rim * sn, rim * c + rre * sn)
        for part in range(4):
            xb[0, pl.ds(part * BLOCK, BLOCK), at(n, CHUNK)] = turned[part].astype(BF16)
            xb[1, pl.ds(part * BLOCK, BLOCK), at(n, CHUNK)] = (
                SWAP_SIGN[part] * turned[part ^ 1]).astype(BF16)
        return carry

    lax.fori_loop(0, 4, solve2, 0)

    def solve3(i, carry):
        n = lax.rem(k // 8 + i, 4)
        new = x_solve(0, xb[0], xb[1], n)
        for u in range(2):
            tiles = block_transpose([new[c * BLOCK:(c + 1) * BLOCK, u * LANES:(u + 1) * LANES]
                                     for c in range(4)])
            for p in range(4):
                send3[at(8 * n + 4 * u + p, BLOCK), :] = tiles[p].astype(BF16)
        send_group(send3, got3, A2A3, n)
        return carry

    lax.fori_loop(0, 4, solve3, 0)
    got3[at(k, BLOCK), :] = send3[at(k, BLOCK), :]

    def sum_send(part, total, phase):
        total[rank] = part[rank]

        def body(i, carry):
            j = lax.rem(rank + i, 8)
            remote(part.at[j], total.at[rank], phase, j // 2, lax.rem(j, 2) * GROUP + k).start()
            return carry

        lax.fori_loop(1, 8, body, 0)

    def sum_up(total, phase):
        wait_on(rs.at[phase], total.at[pl.ds(0, 7)])
        value = total[0].astype(F32)
        for j in range(1, 8):
            value += total[j].astype(F32)
        return value

    sum_send(part0, sum0, SUM0)

    forward2 = remote(lens2, lens2, FWD2, fq + 1 - 2 * core, s)

    @pl.when(mine)
    def _():
        wait_on(rs.at[LENS2], lens2.at[pl.ds(0, ROWS * (SHARDS - 1))])
        forward2.start()

    @pl.when(jnp.logical_not(mine))
    def _():
        forward2.wait_recv()

    def trig2(i, carry):
        terms = lens2[at(i, 128), :].astype(F32)
        value = (terms + turn(terms, -32)) + turn(terms, -64)
        value = jnp.where(lanes(value) < BLOCK, value, 0.0)
        value = value + turn(value, 32)
        value = value + turn(value, 64)
        c, sn = cos_sin(om_h * value)
        cos2[at(i, 128), :] = c
        sin2[at(i, 128), :] = -outer_sign(sn) * sn
        return carry

    lax.fori_loop(0, 8, trig2, 0)

    dist0_send[...] = sum_up(sum0, SUM0).astype(BF16)
    for f in range(4):
        for b in range(2):
            give(dist0_send.at[pl.ds(b * ROWS, ROWS)], dist0.at[rank], DIST0, f, 2 * k + b)

    wait_on(rs.at[A2A3], got3.at[pl.ds(0, BLOCK * (GROUP - 1))])
    y_operands(got3, ya)

    def solve4(n, carry):
        new = y_solve(got3, ya, n)
        product = wt_h * new * turn(new, 64)
        image = product + turn(product, -32)
        for u in range(2):
            packed = image[u * 128:u * 128 + BLOCK]
            block = lanes(packed) // BLOCK
            for a in range(1, 4):
                rows = image[u * 128 + a * BLOCK:u * 128 + (a + 1) * BLOCK]
                packed = jnp.where(block == a, turn(rows, a * BLOCK), packed)
            part1[2 * n + u] = packed.astype(BF16)
        turned = new * cos2[at(n, CHUNK), :] + swap_parts(new) * sin2[at(n, CHUNK), :]
        yb[0, at(n, CHUNK), :] = turned.astype(BF16)
        yb[1, at(n, CHUNK), :] = (swap_parts(turned) * outer_sign(turned)).astype(BF16)
        return carry

    lax.fori_loop(0, 4, solve4, 0)
    sum_send(part1, sum1, SUM1)

    def solve5(i, carry):
        n = lax.rem(s // 16 + i, 4)
        send4[at(n, CHUNK), :] = y_solve(yb.at[0], yb.at[1], n).astype(BF16)

        def body(j, inner):
            t = n * 16 + lax.rem(s + j, 16)

            @pl.when(t != s)
            def _():
                remote(send4.at[at(t, ROWS)], got4.at[at(s, ROWS)], A2A4, fq, t).start()

            return inner

        lax.fori_loop(0, 16, body, 0)
        return carry

    lax.fori_loop(0, 4, solve5, 0)
    got4[at(s, ROWS), :] = send4[at(s, ROWS), :]

    total1 = sum_up(sum1, SUM1)
    for d in range(4):
        dist1_send[d] = turn(total1, d * BLOCK).astype(BF16)

    def go_dist1(i, carry):
        f = i // 8
        a = lax.rem(i, 8) // 2
        b = lax.rem(i, 2)
        d = lax.rem(k + 4 - a, 4)
        give(dist1_send.at[d, at(b, ROWS)], dist1.at[k], DIST1, f, 8 * rank + lax.rem(i, 8))
        return carry

    lax.fori_loop(0, 32, go_dist1, 0)

    loads[4].wait()
    wait_on(rs.at[A2A4], got4.at[pl.ds(0, ROWS * (SHARDS - 1))])

    def gather4(i, carry):
        f = i // 8
        q = lax.rem(i, 8)
        tiles = block_transpose([got4[at(f * GROUP + 4 * q + p, ROWS), :].astype(F32) for p in range(4)])
        for c in range(4):
            xf[f, 0, pl.ds(c * ROWS, ROWS), at(q, LANES)] = tiles[c].astype(BF16)
            xf[f, 1, pl.ds(c * ROWS, ROWS), at(q, LANES)] = (SWAP_SIGN[c] * tiles[c ^ 1]).astype(BF16)
        return carry

    lax.fori_loop(0, 16, gather4, 0)

    def solve6(n, carry):
        image = jnp.zeros((ROWS, CHUNK), F32)
        for f in range(2):
            which = jnp.where(h == f, 0, 1)
            new = x_solve(which, xf[f, 0], xf[f, 1], n)
            sre, sim, rre, rim = (new[c * ROWS:(c + 1) * ROWS] for c in range(4))
            src_out[0, f, :, at(n, CHUNK)] = sre.astype(BF16)
            src_out[1, f, :, at(n, CHUNK)] = sim.astype(BF16)
            rcv_out[0, f, :, at(n, CHUNK)] = rre.astype(BF16)
            rcv_out[1, f, :, at(n, CHUNK)] = rim.astype(BF16)
            image += wt[f] * (sre * rre + sim * rim)
        pair[core, :, at(n, CHUNK)] = image.astype(BF16)
        return carry

    lax.fori_loop(0, 4, solve6, 0)
    to_pair = remote(pair.at[core], pair.at[core], PAIR, fq + 1 - 2 * core, s)
    to_pair.start()

    wait_on(rs.at[DIST0], dist0)
    wait_on(rs.at[DIST1], dist1)
    for j in range(8):
        grad[0, :, pl.ds(j * LANES, LANES)] = dist0[j].astype(F32)
        tile = dist1[4 * j].astype(F32)
        block = lanes(tile) // BLOCK
        for p in range(1, 4):
            tile = jnp.where(block == p, dist1[4 * j + p].astype(F32), tile)
        grad[1, :, pl.ds(j * LANES, LANES)] = tile

    to_pair.wait_recv()
    cross[z_hi] = (pair[0].astype(F32) + pair[1].astype(F32)).astype(BF16)
    to_cross = remote(cross.at[z_hi], cross.at[z_hi], CROSS, lax.rem(fq + 2, 4), s)
    to_cross.start()

    wait_on(ss.at[A2A1], send1.at[pl.ds(0, ROWS * (SHARDS - 1))])
    wait_on(ss.at[A2A2], send2.at[pl.ds(0, BLOCK * (GROUP - 1))])
    wait_on(ss.at[A2A3], send3.at[pl.ds(0, BLOCK * (GROUP - 1))])
    wait_on(ss.at[A2A4], send4.at[pl.ds(0, ROWS * (SHARDS - 1))])
    wait_on(ss.at[SUM0], part0.at[pl.ds(0, 7)])
    wait_on(ss.at[SUM1], part1.at[pl.ds(0, 7)])
    forward1.wait_send()

    own1 = (s == 0) | (s == SHARDS - 1)

    @pl.when(mine & own1)
    def _():
        wait_on(ss.at[LENS1], lens_v.at[1])

    @pl.when(mine & jnp.logical_not(own1))
    def _():
        wait_on(ss.at[LENS1], lens_v.at[pl.ds(0, 2)])

    @pl.when(mine)
    def _():
        wait_on(ss.at[LENS2], lens2_send.at[pl.ds(0, ROWS * 31)])
        forward2.wait_send()

    @pl.when(jnp.logical_not(mine))
    def _():
        wait_on(ss.at[LENS2], lens2_send)

    @pl.when(own1)
    def _():
        wait_on(ss.at[DIST0], dist0.at[pl.ds(0, 7)])

    @pl.when(jnp.logical_not(own1))
    def _():
        wait_on(ss.at[DIST0], dist0)

    own_dist = s // 8 == rank

    @pl.when(own_dist)
    def _():
        wait_on(ss.at[DIST1], dist1.at[pl.ds(0, 31)])

    @pl.when(jnp.logical_not(own_dist))
    def _():
        wait_on(ss.at[DIST1], dist1)

    to_pair.wait_send()
    to_cross.wait()
    grad[2] = cross[0].astype(F32) + cross[1].astype(F32)


def on_device(source_field, receiver_field, line_inverse, lens_delay, omegas, image_weights):
    vmem = pltpu.VMEM
    plane = vmem((NL, LANES), BF16)
    return pl.pallas_call(
        kernel,
        out_shape=(
            jax.ShapeDtypeStruct(source_field.shape, BF16),
            jax.ShapeDtypeStruct(receiver_field.shape, BF16),
            jax.ShapeDtypeStruct(lens_delay.shape, F32),
        ),
        in_specs=[pl.BlockSpec(memory_space=pl.ANY)] * 4 + [pl.BlockSpec(memory_space=pltpu.SMEM)] * 2,
        out_specs=[pl.BlockSpec(memory_space=vmem)] * 3,
        scratch_shapes=[
            vmem(source_field.shape, BF16), vmem(receiver_field.shape, BF16), vmem(lens_delay.shape, F32),
            vmem((2, 2, NL, NL), BF16),
            plane, plane, plane, plane, plane, plane, plane, plane,
            plane, vmem((2, NL, LANES), BF16),
            vmem((2, LANES, NL), BF16), vmem((2, LANES, NL), BF16), vmem((2, 2, 64, NL), BF16),
            vmem((BLOCK, NL), F32), vmem((BLOCK, NL), F32),
            vmem((NL, LANES), F32), vmem((NL, LANES), F32),
            vmem((2, ROWS, NL), F32), vmem((GROUP * ROWS, LANES), BF16), plane,
            vmem((8, BLOCK, LANES), BF16), vmem((8, BLOCK, LANES), BF16),
            vmem((BLOCK, LANES), BF16), vmem((8, ROWS, LANES), BF16),
            vmem((8, BLOCK, LANES), BF16), vmem((8, BLOCK, LANES), BF16),
            vmem((4, BLOCK, LANES), BF16), vmem((GROUP, ROWS, LANES), BF16),
            vmem((2, ROWS, NL), BF16), vmem((2, ROWS, NL), BF16),
            pltpu.SemaphoreType.DMA((5,)),
            pltpu.SemaphoreType.DMA((PHASES,)),
            pltpu.SemaphoreType.DMA((PHASES,)),
        ],
        compiler_params=pltpu.CompilerParams(
            collective_id=0, has_side_effects=True, vmem_limit_bytes=40 * 2**20),
    )(source_field, receiver_field, line_inverse, lens_delay, omegas, image_weights)


def solution(mesh):
    placed = (
        P(None, "freq", "space", None),
        P(None, "freq", "space", None),
        P(None, "freq", None, None),
        P(None, "space", None),
        P("freq"),
        P("freq"),
    )
    return jax.shard_map(
        on_device,
        mesh=mesh,
        in_specs=placed,
        out_specs=(
            P(None, "freq", "space", None),
            P(None, "freq", "space", None),
            P(None, "space", None),
        ),
        check_vma=False,
    )
```

```python
import jax
import jax.numpy as jnp
from jax import lax
from jax.experimental import pallas as pl
from jax.experimental.pallas import tpu as pltpu
from jax.sharding import PartitionSpec as P

F32 = jnp.float32
BF16 = jnp.bfloat16
MESH = pl.DeviceIdType.MESH
LANES = 128
BLOCK = 32
NL = 1024
ROWS = 16
GROUP = 32
SHARDS = 64
CHUNK = 256
SWAP_SIGN = (-1.0, 1.0, 1.0, -1.0)

(A2A1, A2A2, A2A3, A2A4, LENS1, LENS2, FWD1, FWD2,
 SUM0, DIST0, SUM1, DIST1, PAIR, _, _, _, CROSS, _, _, _) = range(20)
PHASES = 20


def lanes(tile):
    return lax.broadcasted_iota(jnp.int32, tile.shape, 1)


def turn(tile, shift):
    return pltpu.roll(tile, shift % LANES, 1)


def even_block(tile):
    return (lanes(tile) // BLOCK) % 2 == 0


def block_transpose(tiles):
    t0, t1, t2, t3 = tiles
    low = lanes(t0) < 64
    even = even_block(t0)
    a0, a2 = jnp.where(low, t0, turn(t2, 64)), jnp.where(low, turn(t0, 64), t2)
    a1, a3 = jnp.where(low, t1, turn(t3, 64)), jnp.where(low, turn(t1, 64), t3)
    b0, b1 = jnp.where(even, a0, turn(a1, 32)), jnp.where(even, turn(a0, -32), a1)
    b2, b3 = jnp.where(even, a2, turn(a3, 32)), jnp.where(even, turn(a2, -32), a3)
    return b0, b1, b2, b3


def swap_parts(tile):
    return jnp.where(even_block(tile), turn(tile, -32), turn(tile, 32))


def outer_sign(tile):
    block = lanes(tile) // BLOCK
    return jnp.where((block == 0) | (block == 3), -1.0, 1.0)


def cos_sin(theta):
    n = jnp.floor(theta * 0.3183098861837907 + 0.5)
    r = theta - n * 3.140625
    r = r - n * 9.67502593994140625e-4
    r = r - n * 1.509957990978376e-7
    flip = 1.0 - 2.0 * (n - 2.0 * jnp.floor(n * 0.5))
    z = r * r
    s = -1.0 / 39916800.0
    for term in (1.0 / 362880.0, -1.0 / 5040.0, 1.0 / 120.0, -1.0 / 6.0, 1.0):
        s = s * z + term
    c = 1.0 / 479001600.0
    for term in (-1.0 / 3628800.0, 1.0 / 40320.0, -1.0 / 720.0, 1.0 / 24.0, -0.5, 1.0):
        c = c * z + term
    return c * flip, s * r * flip


def at(index, size):
    start = index * size
    return pl.ds(start if isinstance(start, int) else pl.multiple_of(start, size), size)


def kernel(src, rcv, minv, lens, om_hbm, wt_hbm, src_out, rcv_out, grad,
           src_v, rcv_v, lens_v, m, mt, send1, got1, send2, got2, send3, got3, send4, got4,
           ya, yb, xa, xb, xf, cos1, sin1, cos2, sin2, lens1, lens2_send, lens2,
           part0, sum0, dist0_send, dist0, part1, sum1, dist1_send, dist1,
           pair, cross, om, wt, load_sem, ss, rs):
    fq = lax.axis_index("freq")
    s = lax.axis_index("space")
    h = s // GROUP
    k = lax.rem(s, GROUP)
    core = lax.rem(fq, 2)
    z_hi = fq // 2
    rank = 2 * fq + h
    mine = lax.rem(s, 2) == core

    def remote(source, target, phase, freq, space):
        return pltpu.make_async_remote_copy(
            src_ref=source, dst_ref=target, send_sem=ss.at[phase], recv_sem=rs.at[phase],
            device_id={"freq": freq, "space": space}, device_id_type=MESH)

    def wait_on(sem, ref):
        pltpu.make_async_copy(ref, ref, sem).wait()

    def give(source, target, phase, freq, space):
        here = (freq == fq) & (space == s)

        @pl.when(here)
        def _():
            pltpu.make_async_copy(source, target, rs.at[phase]).start()

        @pl.when(jnp.logical_not(here))
        def _():
            remote(source, target, phase, freq, space).start()

    loads = [
        pltpu.make_async_copy(src, src_v, load_sem.at[0]),
        pltpu.make_async_copy(rcv, rcv_v, load_sem.at[1]),
        pltpu.make_async_copy(lens, lens_v, load_sem.at[2]),
        pltpu.make_async_copy(om_hbm, om, load_sem.at[5]),
        pltpu.make_async_copy(wt_hbm, wt, load_sem.at[6]),
        pltpu.make_async_copy(minv.at[:, h], m.at[0], load_sem.at[3]),
        pltpu.make_async_copy(minv.at[:, 1 - h], m.at[1], load_sem.at[4]),
    ]
    for load in loads:
        load.start()
    barrier = pltpu.get_barrier_semaphore()
    pending = []
    own1 = (s == 0) | (s == SHARDS - 1)

    def sent(phase, ref, condition=None):
        def wait():
            if condition is None:
                wait_on(ss.at[phase], ref)
            else:
                pl.when(condition)(lambda: wait_on(ss.at[phase], ref))

        pending.append(wait)


    def greet(i, carry):
        pl.semaphore_signal(barrier, inc=1, device_id={"freq": fq, "space": lax.rem(s + i, SHARDS)},
                            device_id_type=MESH)
        return carry

    lax.fori_loop(1, SHARDS, greet, 0)
    for i in range(1, 4):
        pl.semaphore_signal(barrier, inc=1, device_id={"freq": lax.rem(fq + i, 4), "space": s},
                            device_id_type=MESH)
    for load in loads[:5]:
        load.wait()
    om_h = om[h]
    wt_h = wt[h]

    def rotate0(i, carry):
        f = i // 8
        q = lax.rem(i, 8)
        c, sn = cos_sin(om[f] * lens_v[0, :, at(q, LANES)])
        sre = src_v[0, f, :, at(q, LANES)].astype(F32)
        sim = src_v[1, f, :, at(q, LANES)].astype(F32)
        rre = rcv_v[0, f, :, at(q, LANES)].astype(F32)
        rim = rcv_v[1, f, :, at(q, LANES)].astype(F32)
        tiles = block_transpose((sre * c + sim * sn, sim * c - sre * sn,
                                 rre * c - rim * sn, rim * c + rre * sn))
        for p in range(4):
            send1[at(f * GROUP + 4 * q + p, ROWS), :] = tiles[p].astype(BF16)
        return carry

    lax.fori_loop(0, 16, rotate0, 0)
    got1[at(s, ROWS), :] = send1[at(s, ROWS), :]
    pl.semaphore_wait(barrier, SHARDS - 1 + 3)

    def go1(i, carry):
        t = lax.rem(s + i, SHARDS)
        remote(send1.at[at(t, ROWS)], got1.at[at(s, ROWS)], A2A1, fq, t).start()
        return carry

    lax.fori_loop(1, SHARDS, go1, 0)
    sent(A2A1, send1.at[pl.ds(0, ROWS * (SHARDS - 1))])

    @pl.when(mine)
    def _():
        for half in range(2):
            give(lens_v.at[1], lens1.at[core], LENS1, fq, half * GROUP + s // 2)

    sent(LENS1, lens_v.at[1], mine & own1)
    sent(LENS1, lens_v.at[pl.ds(0, 2)], mine & jnp.logical_not(own1))

    def pack2(q, carry):
        value = lens_v[2, :, at(q, LANES)]
        high = value.astype(BF16).astype(F32)
        rest = value - high
        middle = rest.astype(BF16).astype(F32)
        tiles = block_transpose((high, middle, rest - middle, jnp.zeros_like(value)))
        for p in range(4):
            lens2_send[at(4 * q + p, ROWS), :] = tiles[p].astype(BF16)
        return carry

    lax.fori_loop(0, 8, pack2, 0)

    def y_operands(got, other):
        def body(i, carry):
            tile = got[at(i, 128), :].astype(F32)
            other[at(i, 128), :] = (swap_parts(tile) * outer_sign(tile)).astype(BF16)
            return carry

        lax.fori_loop(0, 8, body, 0)

    def y_solve(first, second, n):
        rows = at(n, CHUNK)
        return (jnp.dot(m[0, 0, rows, :], first[...], preferred_element_type=F32)
                + jnp.dot(m[0, 1, rows, :], second[...], preferred_element_type=F32))

    def x_solve(f, first, second, n):
        columns = at(n, CHUNK)
        return (jnp.dot(first, mt[f, 0, :, columns], preferred_element_type=F32)
                + jnp.dot(second, mt[f, 1, :, columns], preferred_element_type=F32))

    def flip_matrix(f):
        def body(i, carry):
            part = i // 8
            r = lax.rem(i, 8)
            mt[f, part, :, at(r, LANES)] = m[f, part, at(r, LANES), :].T
            return carry

        lax.fori_loop(0, 16, body, 0)

    def send_group(send, got, phase, n):
        def body(i, carry):
            t = n * 8 + lax.rem(k + i, 8)

            @pl.when(t != k)
            def _():
                remote(send.at[at(t, BLOCK)], got.at[at(k, BLOCK)], phase, fq, h * GROUP + t).start()

            return carry

        lax.fori_loop(0, 8, body, 0)

    loads[5].wait()
    flip_matrix(0)
    wait_on(rs.at[A2A1], got1.at[pl.ds(0, ROWS * (SHARDS - 1))])
    y_operands(got1, ya)

    def solve1(i, carry):
        n = lax.rem(k // 8 + i, 4)
        send2[at(n, CHUNK), :] = y_solve(got1, ya, n).astype(BF16)
        send_group(send2, got2, A2A2, n)
        return carry

    lax.fori_loop(0, 4, solve1, 0)
    sent(A2A2, send2.at[pl.ds(0, BLOCK * (GROUP - 1))])
    got2[at(k, BLOCK), :] = send2[at(k, BLOCK), :]

    wait_on(rs.at[LENS1], lens1.at[0])
    forward1 = remote(lens1.at[core], lens1.at[core], FWD1, fq + 1 - 2 * core, s)
    forward1.start()
    pending.append(forward1.wait_send)

    skew = jnp.where(mine, 0, 1)

    def go_lens2(i, carry):
        t = lax.rem(s + skew + 2 * i, SHARDS)

        @pl.when(t != s)
        def _():
            remote(lens2_send.at[at(lax.rem(t, GROUP), ROWS)], lens2.at[at(s, ROWS)], LENS2, fq, t).start()

        return carry

    lax.fori_loop(0, 32, go_lens2, 0)
    sent(LENS2, lens2_send.at[pl.ds(0, ROWS * 31)], mine)
    sent(LENS2, lens2_send, jnp.logical_not(mine))

    @pl.when(mine)
    def _():
        lens2[at(s, ROWS), :] = lens2_send[at(k, ROWS), :]

    forward1.wait_recv()

    def trig1(q, carry):
        for b in range(2):
            c, sn = cos_sin(om_h * lens1[b, :, at(q, LANES)])
            cos1[pl.ds(b * ROWS, ROWS), at(q, LANES)] = c
            sin1[pl.ds(b * ROWS, ROWS), at(q, LANES)] = sn
        return carry

    lax.fori_loop(0, 8, trig1, 0)

    wait_on(rs.at[A2A2], got2.at[pl.ds(0, BLOCK * (GROUP - 1))])

    def gather2(q, carry):
        tiles = block_transpose([got2[at(4 * q + p, BLOCK), :].astype(F32) for p in range(4)])
        for c in range(4):
            xa[0, pl.ds(c * BLOCK, BLOCK), at(q, LANES)] = tiles[c].astype(BF16)
            xa[1, pl.ds(c * BLOCK, BLOCK), at(q, LANES)] = (SWAP_SIGN[c] * tiles[c ^ 1]).astype(BF16)
        return carry

    lax.fori_loop(0, 8, gather2, 0)

    def solve2(n, carry):
        new = x_solve(0, xa[0], xa[1], n)
        sre, sim, rre, rim = (new[c * BLOCK:(c + 1) * BLOCK] for c in range(4))
        image = wt_h * (sre * rre + sim * rim)
        for u in range(2):
            part0[2 * n + u] = image[:, u * LANES:(u + 1) * LANES].astype(BF16)
        c, sn = cos1[:, at(n, CHUNK)], sin1[:, at(n, CHUNK)]
        turned = (sre * c + sim * sn, sim * c - sre * sn, rre * c - rim * sn, rim * c + rre * sn)
        for part in range(4):
            xb[0, pl.ds(part * BLOCK, BLOCK), at(n, CHUNK)] = turned[part].astype(BF16)
            xb[1, pl.ds(part * BLOCK, BLOCK), at(n, CHUNK)] = (
                SWAP_SIGN[part] * turned[part ^ 1]).astype(BF16)
        return carry

    lax.fori_loop(0, 4, solve2, 0)

    def solve3(i, carry):
        n = lax.rem(k // 8 + i, 4)
        new = x_solve(0, xb[0], xb[1], n)
        for u in range(2):
            tiles = block_transpose([new[c * BLOCK:(c + 1) * BLOCK, u * LANES:(u + 1) * LANES]
                                     for c in range(4)])
            for p in range(4):
                send3[at(8 * n + 4 * u + p, BLOCK), :] = tiles[p].astype(BF16)
        send_group(send3, got3, A2A3, n)
        return carry

    lax.fori_loop(0, 4, solve3, 0)
    sent(A2A3, send3.at[pl.ds(0, BLOCK * (GROUP - 1))])
    got3[at(k, BLOCK), :] = send3[at(k, BLOCK), :]

    def sum_send(part, total, phase):
        total[rank] = part[rank]

        def body(i, carry):
            j = lax.rem(rank + i, 8)
            remote(part.at[j], total.at[rank], phase, j // 2, lax.rem(j, 2) * GROUP + k).start()
            return carry

        lax.fori_loop(1, 8, body, 0)
        sent(phase, part.at[pl.ds(0, 7)])

    def sum_up(total, phase):
        wait_on(rs.at[phase], total.at[pl.ds(0, 7)])
        value = total[0].astype(F32)
        for j in range(1, 8):
            value += total[j].astype(F32)
        return value

    sum_send(part0, sum0, SUM0)

    forward2 = remote(lens2, lens2, FWD2, fq + 1 - 2 * core, s)

    @pl.when(mine)
    def _():
        wait_on(rs.at[LENS2], lens2.at[pl.ds(0, ROWS * (SHARDS - 1))])
        forward2.start()

    @pl.when(jnp.logical_not(mine))
    def _():
        forward2.wait_recv()

    sent(FWD2, lens2, mine)

    def trig2(i, carry):
        terms = lens2[at(i, 128), :].astype(F32)
        value = (terms + turn(terms, -32)) + turn(terms, -64)
        value = jnp.where(lanes(value) < BLOCK, value, 0.0)
        value = value + turn(value, 32)
        value = value + turn(value, 64)
        c, sn = cos_sin(om_h * value)
        cos2[at(i, 128), :] = c
        sin2[at(i, 128), :] = -outer_sign(sn) * sn
        return carry

    lax.fori_loop(0, 8, trig2, 0)

    wait_on(rs.at[A2A3], got3.at[pl.ds(0, BLOCK * (GROUP - 1))])
    y_operands(got3, ya)

    def solve4(n, carry):
        new = y_solve(got3, ya, n)
        product = wt_h * new * turn(new, 64)
        image = product + turn(product, -32)
        for u in range(2):
            packed = image[u * 128:u * 128 + BLOCK]
            block = lanes(packed) // BLOCK
            for a in range(1, 4):
                rows = image[u * 128 + a * BLOCK:u * 128 + (a + 1) * BLOCK]
                packed = jnp.where(block == a, turn(rows, a * BLOCK), packed)
            part1[2 * n + u] = packed.astype(BF16)
        turned = new * cos2[at(n, CHUNK), :] + swap_parts(new) * sin2[at(n, CHUNK), :]
        yb[0, at(n, CHUNK), :] = turned.astype(BF16)
        yb[1, at(n, CHUNK), :] = (swap_parts(turned) * outer_sign(turned)).astype(BF16)
        return carry

    lax.fori_loop(0, 4, solve4, 0)
    sum_send(part1, sum1, SUM1)

    def solve5(i, carry):
        n = lax.rem(s // 16 + i, 4)
        send4[at(n, CHUNK), :] = y_solve(yb.at[0], yb.at[1], n).astype(BF16)

        def body(j, inner):
            t = n * 16 + lax.rem(s + j, 16)

            @pl.when(t != s)
            def _():
                remote(send4.at[at(t, ROWS)], got4.at[at(s, ROWS)], A2A4, fq, t).start()

            return inner

        lax.fori_loop(0, 16, body, 0)
        return carry

    lax.fori_loop(0, 4, solve5, 0)
    sent(A2A4, send4.at[pl.ds(0, ROWS * (SHARDS - 1))])
    got4[at(s, ROWS), :] = send4[at(s, ROWS), :]

    dist0_send[...] = sum_up(sum0, SUM0).astype(BF16)
    for f in range(4):
        for b in range(2):
            give(dist0_send.at[pl.ds(b * ROWS, ROWS)], dist0.at[rank], DIST0, f, 2 * k + b)
    sent(DIST0, dist0.at[pl.ds(0, 7)], own1)
    sent(DIST0, dist0, jnp.logical_not(own1))

    total1 = sum_up(sum1, SUM1)
    for d in range(4):
        dist1_send[d] = turn(total1, d * BLOCK).astype(BF16)

    def go_dist1(i, carry):
        f = i // 8
        a = lax.rem(i, 8) // 2
        b = lax.rem(i, 2)
        d = lax.rem(k + 4 - a, 4)
        give(dist1_send.at[d, at(b, ROWS)], dist1.at[k], DIST1, f, 8 * rank + lax.rem(i, 8))
        return carry

    lax.fori_loop(0, 32, go_dist1, 0)
    sent(DIST1, dist1.at[pl.ds(0, 31)], s // 8 == rank)
    sent(DIST1, dist1, s // 8 != rank)

    loads[6].wait()
    flip_matrix(1)
    wait_on(rs.at[A2A4], got4.at[pl.ds(0, ROWS * (SHARDS - 1))])

    def gather4(i, carry):
        f = i // 8
        q = lax.rem(i, 8)
        tiles = block_transpose([got4[at(f * GROUP + 4 * q + p, ROWS), :].astype(F32) for p in range(4)])
        for c in range(4):
            xf[f, 0, pl.ds(c * ROWS, ROWS), at(q, LANES)] = tiles[c].astype(BF16)
            xf[f, 1, pl.ds(c * ROWS, ROWS), at(q, LANES)] = (SWAP_SIGN[c] * tiles[c ^ 1]).astype(BF16)
        return carry

    lax.fori_loop(0, 16, gather4, 0)

    def pair_copy(n):
        return remote(pair.at[n, core], pair.at[n, core], PAIR + n, fq + 1 - 2 * core, s)

    def cross_copy(n):
        return remote(cross.at[n, z_hi], cross.at[n, z_hi], CROSS + n, lax.rem(fq + 2, 4), s)

    def pass_on(n):
        pair_copy(n).wait_recv()
        cross[n, z_hi] = (pair[n, 0].astype(F32) + pair[n, 1].astype(F32)).astype(BF16)
        cross_copy(n).start()
        pending.append(pair_copy(n).wait_send)
        pending.append(cross_copy(n).wait_send)

    for n in range(4):
        image = jnp.zeros((ROWS, CHUNK), F32)
        for u in range(2):
            f = h if u == 0 else 1 - h
            new = x_solve(u, xf[f, 0], xf[f, 1], n)
            sre, sim, rre, rim = (new[c * ROWS:(c + 1) * ROWS] for c in range(4))
            src_out[0, f, :, at(n, CHUNK)] = sre.astype(BF16)
            src_out[1, f, :, at(n, CHUNK)] = sim.astype(BF16)
            rcv_out[0, f, :, at(n, CHUNK)] = rre.astype(BF16)
            rcv_out[1, f, :, at(n, CHUNK)] = rim.astype(BF16)
            image += wt[f] * (sre * rre + sim * rim)
        pair[n, core] = image.astype(BF16)
        pair_copy(n).start()
        if n > 0:
            pass_on(n - 1)
    pass_on(3)

    wait_on(rs.at[DIST0], dist0)
    wait_on(rs.at[DIST1], dist1)
    for j in range(8):
        grad[0, :, pl.ds(j * LANES, LANES)] = dist0[j].astype(F32)
        tile = dist1[4 * j].astype(F32)
        block = lanes(tile) // BLOCK
        for p in range(1, 4):
            tile = jnp.where(block == p, dist1[4 * j + p].astype(F32), tile)
        grad[1, :, pl.ds(j * LANES, LANES)] = tile

    for wait in pending:
        wait()

    for n in range(4):
        cross_copy(n).wait_recv()
        grad[2, :, at(n, CHUNK)] = cross[n, 0].astype(F32) + cross[n, 1].astype(F32)


def on_device(source_field, receiver_field, line_inverse, lens_delay, omegas, image_weights):
    vmem = pltpu.VMEM
    plane = vmem((NL, LANES), BF16)
    return pl.pallas_call(
        kernel,
        out_shape=(
            vmem(source_field.shape, BF16),
            vmem(receiver_field.shape, BF16),
            vmem(lens_delay.shape, F32),
        ),
        in_specs=[pl.BlockSpec(memory_space=pl.ANY)] * 6,
        out_specs=[pl.BlockSpec(memory_space=vmem)] * 3,
        scratch_shapes=[
            vmem(source_field.shape, BF16), vmem(receiver_field.shape, BF16), vmem(lens_delay.shape, F32),
            vmem((2, 2, NL, NL), BF16), vmem((2, 2, NL, NL), BF16),
            plane, plane, plane, plane, plane, plane, plane, plane,
            plane, vmem((2, NL, LANES), BF16),
            vmem((2, LANES, NL), BF16), vmem((2, LANES, NL), BF16), vmem((2, 2, 64, NL), BF16),
            vmem((BLOCK, NL), F32), vmem((BLOCK, NL), F32),
            vmem((NL, LANES), F32), vmem((NL, LANES), F32),
            vmem((2, ROWS, NL), F32), vmem((GROUP * ROWS, LANES), BF16), plane,
            vmem((8, BLOCK, LANES), BF16), vmem((8, BLOCK, LANES), BF16),
            vmem((BLOCK, LANES), BF16), vmem((8, ROWS, LANES), BF16),
            vmem((8, BLOCK, LANES), BF16), vmem((8, BLOCK, LANES), BF16),
            vmem((4, BLOCK, LANES), BF16), vmem((GROUP, ROWS, LANES), BF16),
            vmem((4, 2, ROWS, CHUNK), BF16), vmem((4, 2, ROWS, CHUNK), BF16),
            pltpu.SMEM((2,), F32), pltpu.SMEM((2,), F32),
            pltpu.SemaphoreType.DMA((7,)),
            pltpu.SemaphoreType.DMA((PHASES,)),
            pltpu.SemaphoreType.DMA((PHASES,)),
        ],
        compiler_params=pltpu.CompilerParams(
            collective_id=0, has_side_effects=True, vmem_limit_bytes=60 * 2**20),
    )(source_field, receiver_field, line_inverse, lens_delay, omegas, image_weights)


def solution(mesh):
    placed = (
        P(None, "freq", "space", None),
        P(None, "freq", "space", None),
        P(None, "freq", None, None),
        P(None, "space", None),
        P("freq"),
        P("freq"),
    )
    return jax.shard_map(
        on_device,
        mesh=mesh,
        in_specs=placed,
        out_specs=(
            P(None, "freq", "space", None),
            P(None, "freq", "space", None),
            P(None, "space", None),
        ),
        check_vma=False,
    )
```

```python
import jax
import jax.numpy as jnp
from jax import lax
from jax.experimental import pallas as pl
from jax.experimental.pallas import tpu as pltpu
from jax.sharding import PartitionSpec as P

F32 = jnp.float32
BF16 = jnp.bfloat16
MESH = pl.DeviceIdType.MESH
LANES = 128
BLOCK = 32
NL = 1024
ROWS = 16
GROUP = 32
SHARDS = 64
CHUNK = 256
SWAP_SIGN = (-1.0, 1.0, 1.0, -1.0)

(A2A1, A2A2, A2A3, A2A4, LENS1, LENS2, FWD1, FWD2,
 SUM0, DIST0, SUM1, DIST1, PAIR, _, _, _, CROSS, _, _, _) = range(20)
PHASES = 20


def lanes(tile):
    return lax.broadcasted_iota(jnp.int32, tile.shape, 1)


def turn(tile, shift):
    return pltpu.roll(tile, shift % LANES, 1)


def even_block(tile):
    return (lanes(tile) // BLOCK) % 2 == 0


def block_transpose(tiles):
    t0, t1, t2, t3 = tiles
    low = lanes(t0) < 64
    even = even_block(t0)
    a0, a2 = jnp.where(low, t0, turn(t2, 64)), jnp.where(low, turn(t0, 64), t2)
    a1, a3 = jnp.where(low, t1, turn(t3, 64)), jnp.where(low, turn(t1, 64), t3)
    b0, b1 = jnp.where(even, a0, turn(a1, 32)), jnp.where(even, turn(a0, -32), a1)
    b2, b3 = jnp.where(even, a2, turn(a3, 32)), jnp.where(even, turn(a2, -32), a3)
    return b0, b1, b2, b3


def swap_parts(tile):
    return jnp.where(even_block(tile), turn(tile, -32), turn(tile, 32))


def outer_sign(tile):
    block = lanes(tile) // BLOCK
    return jnp.where((block == 0) | (block == 3), -1.0, 1.0)


def cos_sin(theta):
    n = jnp.floor(theta * 0.3183098861837907 + 0.5)
    r = theta - n * 3.140625
    r = r - n * 9.67502593994140625e-4
    r = r - n * 1.509957990978376e-7
    flip = 1.0 - 2.0 * (n - 2.0 * jnp.floor(n * 0.5))
    z = r * r
    s = -1.0 / 39916800.0
    for term in (1.0 / 362880.0, -1.0 / 5040.0, 1.0 / 120.0, -1.0 / 6.0, 1.0):
        s = s * z + term
    c = 1.0 / 479001600.0
    for term in (-1.0 / 3628800.0, 1.0 / 40320.0, -1.0 / 720.0, 1.0 / 24.0, -0.5, 1.0):
        c = c * z + term
    return c * flip, s * r * flip


def at(index, size):
    start = index * size
    return pl.ds(start if isinstance(start, int) else pl.multiple_of(start, size), size)


def kernel(src, rcv, minv, lens, om_hbm, wt_hbm, fields, grad,
           src_v, rcv_v, lens_v, m, mt, send1, got1, send2, got2, send3, got3, send4, got4,
           ya, yb, xa, xb, xf, acc_y, acc_x, acc_f, cos1, sin1, cos2, sin2, lens1, lens2_send, lens2,
           part0, sum0, dist0_send, dist0, part1, sum1, dist1_send, dist1,
           pair, cross, om, wt, load_sem, ss, rs, parts):
    src_out, rcv_out = fields.at[0], fields.at[1]
    fq = lax.axis_index("freq")
    s = lax.axis_index("space")
    h = s // GROUP
    k = lax.rem(s, GROUP)
    core = lax.rem(fq, 2)
    z_hi = fq // 2
    rank = 2 * fq + h
    mine = lax.rem(s, 2) == core

    def remote(source, target, phase, freq, space):
        return pltpu.make_async_remote_copy(
            src_ref=source, dst_ref=target, send_sem=ss.at[phase], recv_sem=rs.at[phase],
            device_id={"freq": freq, "space": space}, device_id_type=MESH)

    quarter = k // 8
    plane = s // 16

    def transposed(source, target, phase, part, space):
        pltpu.make_async_remote_copy(
            src_ref=source, dst_ref=target, send_sem=ss.at[phase], recv_sem=parts.at[4 * phase + part],
            device_id={"freq": fq, "space": space}, device_id_type=MESH).start()

    def wait_on(sem, ref):
        pltpu.make_async_copy(ref, ref, sem).wait()

    def give(source, target, phase, freq, space):
        here = (freq == fq) & (space == s)

        @pl.when(here)
        def _():
            pltpu.make_async_copy(source, target, rs.at[phase]).start()

        @pl.when(jnp.logical_not(here))
        def _():
            remote(source, target, phase, freq, space).start()

    loads = [
        pltpu.make_async_copy(src, src_v, load_sem.at[0]),
        pltpu.make_async_copy(rcv, rcv_v, load_sem.at[1]),
        pltpu.make_async_copy(lens, lens_v, load_sem.at[2]),
        pltpu.make_async_copy(om_hbm, om, load_sem.at[5]),
        pltpu.make_async_copy(wt_hbm, wt, load_sem.at[6]),
        pltpu.make_async_copy(minv.at[:, h], m.at[0], load_sem.at[3]),
        pltpu.make_async_copy(minv.at[:, 1 - h], m.at[1], load_sem.at[4]),
    ]
    for load in loads:
        load.start()
    barrier = pltpu.get_barrier_semaphore()
    pending = []
    own1 = (s == 0) | (s == SHARDS - 1)

    def sent(phase, ref, condition=None):
        def wait():
            if condition is None:
                wait_on(ss.at[phase], ref)
            else:
                pl.when(condition)(lambda: wait_on(ss.at[phase], ref))

        pending.append(wait)


    def greet(i, carry):
        pl.semaphore_signal(barrier, inc=1, device_id={"freq": fq, "space": lax.rem(s + i, SHARDS)},
                            device_id_type=MESH)
        return carry

    lax.fori_loop(1, SHARDS, greet, 0)
    for i in range(1, 4):
        pl.semaphore_signal(barrier, inc=1, device_id={"freq": lax.rem(fq + i, 4), "space": s},
                            device_id_type=MESH)
    for load in loads[:5]:
        load.wait()
    om_h = om[h]
    wt_h = wt[h]

    def rotate0(i, carry):
        f = i // 8
        q = lax.rem(i, 8)
        c, sn = cos_sin(om[f] * lens_v[0, :, at(q, LANES)])
        sre = src_v[0, f, :, at(q, LANES)].astype(F32)
        sim = src_v[1, f, :, at(q, LANES)].astype(F32)
        rre = rcv_v[0, f, :, at(q, LANES)].astype(F32)
        rim = rcv_v[1, f, :, at(q, LANES)].astype(F32)
        tiles = block_transpose((sre * c + sim * sn, sim * c - sre * sn,
                                 rre * c - rim * sn, rim * c + rre * sn))
        for p in range(4):
            send1[at(f * GROUP + 4 * q + p, ROWS), :] = tiles[p].astype(BF16)
        return carry

    lax.fori_loop(0, 16, rotate0, 0)
    got1[at(s, ROWS), :] = send1[at(s, ROWS), :]
    pl.semaphore_wait(barrier, SHARDS - 1 + 3)

    def send_all(send, got, phase, n):
        def body(i, carry):
            t = n * 16 + lax.rem(s + i, 16)

            @pl.when(t != s)
            def _():
                transposed(send.at[at(t, ROWS)], got.at[at(s, ROWS)], phase, plane, t)

            return carry

        lax.fori_loop(0, 16, body, 0)

    def go1(i, carry):
        send_all(send1, got1, A2A1, lax.rem(plane + i, 4))
        return carry

    lax.fori_loop(0, 4, go1, 0)
    sent(A2A1, send1.at[pl.ds(0, ROWS * (SHARDS - 1))])

    @pl.when(mine)
    def _():
        for half in range(2):
            give(lens_v.at[1], lens1.at[core], LENS1, fq, half * GROUP + s // 2)

    sent(LENS1, lens_v.at[1], mine & own1)
    sent(LENS1, lens_v.at[pl.ds(0, 2)], mine & jnp.logical_not(own1))

    def pack2(q, carry):
        value = lens_v[2, :, at(q, LANES)]
        high = value.astype(BF16).astype(F32)
        rest = value - high
        middle = rest.astype(BF16).astype(F32)
        tiles = block_transpose((high, middle, rest - middle, jnp.zeros_like(value)))
        for p in range(4):
            lens2_send[at(4 * q + p, ROWS), :] = tiles[p].astype(BF16)
        return carry

    lax.fori_loop(0, 8, pack2, 0)

    def arrivals(phase, got, own, lines, use, last):
        for i in range(4):
            g = lax.rem(own + 4 - i, 4)
            wait_on(parts.at[4 * phase + g], got.at[pl.ds(0, CHUNK - (lines if i == 0 else 0))])
            if i < 3:
                use(g, i)
            else:
                last(g)

    def y_operands(got, other, g):
        for u in range(2):
            rows = at(2 * g + u, 128)
            tile = got[rows, :].astype(F32)
            other[rows, :] = (swap_parts(tile) * outer_sign(tile)).astype(BF16)

    def y_arrivals(phase, got, own, lines, start, finish):
        def part(g, rows):
            return (jnp.dot(m[0, 0, rows, at(g, CHUNK)], got[at(g, CHUNK), :], preferred_element_type=F32)
                    + jnp.dot(m[0, 1, rows, at(g, CHUNK)], ya[at(g, CHUNK), :], preferred_element_type=F32))

        def use(g, i):
            y_operands(got, ya, g)

            def body(n, carry):
                rows = at(n, CHUNK)
                acc_y[rows, :] = part(g, rows) if i == 0 else acc_y[rows, :] + part(g, rows)
                return carry

            lax.fori_loop(0, 4, body, 0)

        def last(g):
            y_operands(got, ya, g)

            def body(i, carry):
                n = lax.rem(start + i, 4)
                rows = at(n, CHUNK)
                finish(n, acc_y[rows, :] + part(g, rows))
                return carry

            lax.fori_loop(0, 4, body, 0)

        arrivals(phase, got, own, lines, use, last)

    def y_solve(first, second, n):
        rows = at(n, CHUNK)
        return (jnp.dot(m[0, 0, rows, :], first[...], preferred_element_type=F32)
                + jnp.dot(m[0, 1, rows, :], second[...], preferred_element_type=F32))

    def x_solve(f, first, second, n):
        columns = at(n, CHUNK)
        return (jnp.dot(first, mt[f, 0, :, columns], preferred_element_type=F32)
                + jnp.dot(second, mt[f, 1, :, columns], preferred_element_type=F32))

    def flip_matrix(f, begin, end):
        def body(i, carry):
            part = i // 8
            r = lax.rem(i, 8)
            mt[f, part, :, at(r, LANES)] = m[f, part, at(r, LANES), :].T
            return carry

        lax.fori_loop(begin, end, body, 0)

    def send_group(send, got, phase, n):
        def body(i, carry):
            t = n * 8 + lax.rem(k + i, 8)

            @pl.when(t != k)
            def _():
                transposed(send.at[at(t, BLOCK)], got.at[at(k, BLOCK)], phase, quarter, h * GROUP + t)

            return carry

        lax.fori_loop(0, 8, body, 0)

    loads[5].wait()
    flip_matrix(0, 0, 16)

    def finish1(n, new):
        send2[at(n, CHUNK), :] = new.astype(BF16)
        send_group(send2, got2, A2A2, n)

    y_arrivals(A2A1, got1, plane, ROWS, quarter, finish1)
    sent(A2A2, send2.at[pl.ds(0, BLOCK * (GROUP - 1))])
    got2[at(k, BLOCK), :] = send2[at(k, BLOCK), :]

    wait_on(rs.at[LENS1], lens1.at[0])
    forward1 = remote(lens1.at[core], lens1.at[core], FWD1, fq + 1 - 2 * core, s)
    forward1.start()
    pending.append(forward1.wait_send)

    skew = jnp.where(mine, 0, 1)

    def go_lens2(i, carry):
        t = lax.rem(s + skew + 2 * i, SHARDS)

        @pl.when(t != s)
        def _():
            remote(lens2_send.at[at(lax.rem(t, GROUP), ROWS)], lens2.at[at(s, ROWS)], LENS2, fq, t).start()

        return carry

    lax.fori_loop(0, 32, go_lens2, 0)
    sent(LENS2, lens2_send.at[pl.ds(0, ROWS * 31)], mine)
    sent(LENS2, lens2_send, jnp.logical_not(mine))

    @pl.when(mine)
    def _():
        lens2[at(s, ROWS), :] = lens2_send[at(k, ROWS), :]

    forward1.wait_recv()

    def trig1(q, carry):
        for b in range(2):
            c, sn = cos_sin(om_h * lens1[b, :, at(q, LANES)])
            cos1[pl.ds(b * ROWS, ROWS), at(q, LANES)] = c
            sin1[pl.ds(b * ROWS, ROWS), at(q, LANES)] = sn
        return carry

    lax.fori_loop(0, 8, trig1, 0)
    loads[6].wait()
    flip_matrix(1, 0, 8)

    def gather2(g):
        for u in range(2):
            q = 2 * g + u
            tiles = block_transpose([got2[at(4 * q + p, BLOCK), :].astype(F32) for p in range(4)])
            for c in range(4):
                xa[0, pl.ds(c * BLOCK, BLOCK), at(q, LANES)] = tiles[c].astype(BF16)
                xa[1, pl.ds(c * BLOCK, BLOCK), at(q, LANES)] = (SWAP_SIGN[c] * tiles[c ^ 1]).astype(BF16)

    def x_part(g, columns):
        return (jnp.dot(xa[0, :, at(g, CHUNK)], mt[0, 0, at(g, CHUNK), columns], preferred_element_type=F32)
                + jnp.dot(xa[1, :, at(g, CHUNK)], mt[0, 1, at(g, CHUNK), columns],
                          preferred_element_type=F32))

    def use2(g, i):
        gather2(g)

        def body(n, carry):
            columns = at(n, CHUNK)
            acc_x[:, columns] = x_part(g, columns) if i == 0 else acc_x[:, columns] + x_part(g, columns)
            return carry

        lax.fori_loop(0, 4, body, 0)

    def last2(g):
        gather2(g)

        def body(n, carry):
            solve2(n, acc_x[:, at(n, CHUNK)] + x_part(g, at(n, CHUNK)))
            return carry

        lax.fori_loop(0, 4, body, 0)

    def solve2(n, new):
        sre, sim, rre, rim = (new[c * BLOCK:(c + 1) * BLOCK] for c in range(4))
        image = wt_h * (sre * rre + sim * rim)
        for u in range(2):
            part0[2 * n + u] = image[:, u * LANES:(u + 1) * LANES].astype(BF16)
        c, sn = cos1[:, at(n, CHUNK)], sin1[:, at(n, CHUNK)]
        turned = (sre * c + sim * sn, sim * c - sre * sn, rre * c - rim * sn, rim * c + rre * sn)
        for part in range(4):
            xb[0, pl.ds(part * BLOCK, BLOCK), at(n, CHUNK)] = turned[part].astype(BF16)
            xb[1, pl.ds(part * BLOCK, BLOCK), at(n, CHUNK)] = (
                SWAP_SIGN[part] * turned[part ^ 1]).astype(BF16)

    arrivals(A2A2, got2, quarter, BLOCK, use2, last2)

    def solve3(i, carry):
        n = lax.rem(k // 8 + i, 4)
        new = x_solve(0, xb[0], xb[1], n)
        for u in range(2):
            tiles = block_transpose([new[c * BLOCK:(c + 1) * BLOCK, u * LANES:(u + 1) * LANES]
                                     for c in range(4)])
            for p in range(4):
                send3[at(8 * n + 4 * u + p, BLOCK), :] = tiles[p].astype(BF16)
        send_group(send3, got3, A2A3, n)
        return carry

    lax.fori_loop(0, 4, solve3, 0)
    sent(A2A3, send3.at[pl.ds(0, BLOCK * (GROUP - 1))])
    got3[at(k, BLOCK), :] = send3[at(k, BLOCK), :]

    def sum_send(part, total, phase):
        total[rank] = part[rank]

        def body(i, carry):
            j = lax.rem(rank + i, 8)
            remote(part.at[j], total.at[rank], phase, j // 2, lax.rem(j, 2) * GROUP + k).start()
            return carry

        lax.fori_loop(1, 8, body, 0)
        sent(phase, part.at[pl.ds(0, 7)])

    def sum_up(total, phase):
        wait_on(rs.at[phase], total.at[pl.ds(0, 7)])
        value = total[0].astype(F32)
        for j in range(1, 8):
            value += total[j].astype(F32)
        return value

    sum_send(part0, sum0, SUM0)

    forward2 = remote(lens2, lens2, FWD2, fq + 1 - 2 * core, s)

    @pl.when(mine)
    def _():
        wait_on(rs.at[LENS2], lens2.at[pl.ds(0, ROWS * (SHARDS - 1))])
        forward2.start()

    @pl.when(jnp.logical_not(mine))
    def _():
        forward2.wait_recv()

    sent(FWD2, lens2, mine)

    def trig2(i, carry):
        terms = lens2[at(i, 128), :].astype(F32)
        value = (terms + turn(terms, -32)) + turn(terms, -64)
        value = jnp.where(lanes(value) < BLOCK, value, 0.0)
        value = value + turn(value, 32)
        value = value + turn(value, 64)
        c, sn = cos_sin(om_h * value)
        cos2[at(i, 128), :] = c
        sin2[at(i, 128), :] = -outer_sign(sn) * sn
        return carry

    lax.fori_loop(0, 8, trig2, 0)
    flip_matrix(1, 8, 16)

    def solve4(n, new):
        product = wt_h * new * turn(new, 64)
        image = product + turn(product, -32)
        for u in range(2):
            packed = image[u * 128:u * 128 + BLOCK]
            block = lanes(packed) // BLOCK
            for a in range(1, 4):
                rows = image[u * 128 + a * BLOCK:u * 128 + (a + 1) * BLOCK]
                packed = jnp.where(block == a, turn(rows, a * BLOCK), packed)
            part1[2 * n + u] = packed.astype(BF16)
        turned = new * cos2[at(n, CHUNK), :] + swap_parts(new) * sin2[at(n, CHUNK), :]
        yb[0, at(n, CHUNK), :] = turned.astype(BF16)
        yb[1, at(n, CHUNK), :] = (swap_parts(turned) * outer_sign(turned)).astype(BF16)

    y_arrivals(A2A3, got3, quarter, BLOCK, 0, solve4)
    sum_send(part1, sum1, SUM1)

    def solve5(i, carry):
        n = lax.rem(plane + i, 4)
        send4[at(n, CHUNK), :] = y_solve(yb.at[0], yb.at[1], n).astype(BF16)

        send_all(send4, got4, A2A4, n)
        return carry

    lax.fori_loop(0, 4, solve5, 0)
    sent(A2A4, send4.at[pl.ds(0, ROWS * (SHARDS - 1))])
    got4[at(s, ROWS), :] = send4[at(s, ROWS), :]

    dist0_send[...] = sum_up(sum0, SUM0).astype(BF16)
    for f in range(4):
        for b in range(2):
            give(dist0_send.at[pl.ds(b * ROWS, ROWS)], dist0.at[rank], DIST0, f, 2 * k + b)
    sent(DIST0, dist0.at[pl.ds(0, 7)], own1)
    sent(DIST0, dist0, jnp.logical_not(own1))

    total1 = sum_up(sum1, SUM1)
    for d in range(4):
        dist1_send[d] = turn(total1, d * BLOCK).astype(BF16)

    def go_dist1(i, carry):
        f = i // 8
        a = lax.rem(i, 8) // 2
        b = lax.rem(i, 2)
        d = lax.rem(k + 4 - a, 4)
        give(dist1_send.at[d, at(b, ROWS)], dist1.at[k], DIST1, f, 8 * rank + lax.rem(i, 8))
        return carry

    lax.fori_loop(0, 32, go_dist1, 0)
    sent(DIST1, dist1.at[pl.ds(0, 31)], s // 8 == rank)
    sent(DIST1, dist1, s // 8 != rank)

    acc_f[...] = jnp.zeros_like(acc_f)

    def gather4(g):
        f = g // 2
        for u in range(4):
            q = 4 * lax.rem(g, 2) + u
            tiles = block_transpose([got4[at(f * GROUP + 4 * q + p, ROWS), :].astype(F32) for p in range(4)])
            for c in range(4):
                xf[f, 0, pl.ds(c * ROWS, ROWS), at(q, LANES)] = tiles[c].astype(BF16)
                xf[f, 1, pl.ds(c * ROWS, ROWS), at(q, LANES)] = (SWAP_SIGN[c] * tiles[c ^ 1]).astype(BF16)

    def f_part(g, columns):
        f = g // 2
        which = jnp.where(h == f, 0, 1)
        terms = at(lax.rem(g, 2), 512)
        return (jnp.dot(xf[f, 0, :, terms], mt[which, 0, terms, columns], preferred_element_type=F32)
                + jnp.dot(xf[f, 1, :, terms], mt[which, 1, terms, columns], preferred_element_type=F32))

    def use4(g, i):
        gather4(g)

        def body(n, carry):
            acc_f[g // 2, :, at(n, CHUNK)] += f_part(g, at(n, CHUNK))
            return carry

        lax.fori_loop(0, 4, body, 0)

    def pair_copy(n):
        return remote(pair.at[n, core], pair.at[n, core], PAIR + n, fq + 1 - 2 * core, s)

    def cross_copy(n):
        return remote(cross.at[n, z_hi], cross.at[n, z_hi], CROSS + n, lax.rem(fq + 2, 4), s)

    def pass_on(n):
        pair_copy(n).wait_recv()
        cross[n, z_hi] = (pair[n, 0].astype(F32) + pair[n, 1].astype(F32)).astype(BF16)
        cross_copy(n).start()
        pending.append(pair_copy(n).wait_send)
        pending.append(cross_copy(n).wait_send)

    def last4(g):
        gather4(g)
        for n in range(4):
            image = jnp.zeros((ROWS, CHUNK), F32)
            for u in range(2):
                f = g // 2 if u == 0 else 1 - g // 2
                new = acc_f[f, :, at(n, CHUNK)]
                if u == 0:
                    new += f_part(g, at(n, CHUNK))
                sre, sim, rre, rim = (new[c * ROWS:(c + 1) * ROWS] for c in range(4))
                src_out[0, f, :, at(n, CHUNK)] = sre.astype(BF16)
                src_out[1, f, :, at(n, CHUNK)] = sim.astype(BF16)
                rcv_out[0, f, :, at(n, CHUNK)] = rre.astype(BF16)
                rcv_out[1, f, :, at(n, CHUNK)] = rim.astype(BF16)
                image += wt[f] * (sre * rre + sim * rim)
            pair[n, core] = image.astype(BF16)
            pair_copy(n).start()
            if n > 0:
                pass_on(n - 1)
        pass_on(3)

    arrivals(A2A4, got4, plane, ROWS, use4, last4)

    wait_on(rs.at[DIST0], dist0)
    wait_on(rs.at[DIST1], dist1)
    for j in range(8):
        grad[0, :, pl.ds(j * LANES, LANES)] = dist0[j].astype(F32)
        tile = dist1[4 * j].astype(F32)
        block = lanes(tile) // BLOCK
        for p in range(1, 4):
            tile = jnp.where(block == p, dist1[4 * j + p].astype(F32), tile)
        grad[1, :, pl.ds(j * LANES, LANES)] = tile

    for wait in pending:
        wait()

    for n in range(4):
        cross_copy(n).wait_recv()
        grad[2, :, at(n, CHUNK)] = cross[n, 0].astype(F32) + cross[n, 1].astype(F32)


def on_device(source_field, receiver_field, line_inverse, lens_delay, omegas, image_weights):
    vmem = pltpu.VMEM
    plane = vmem((NL, LANES), BF16)
    fields, gradient = pl.pallas_call(
        kernel,
        out_shape=(
            vmem((2,) + source_field.shape, BF16),
            vmem(lens_delay.shape, F32),
        ),
        in_specs=[pl.BlockSpec(memory_space=pl.ANY)] * 6,
        out_specs=[pl.BlockSpec(memory_space=vmem)] * 2,
        scratch_shapes=[
            vmem(source_field.shape, BF16), vmem(receiver_field.shape, BF16), vmem(lens_delay.shape, F32),
            vmem((2, 2, NL, NL), BF16), vmem((2, 2, NL, NL), BF16),
            plane, plane, plane, plane, plane, plane, plane, plane,
            plane, vmem((2, NL, LANES), BF16),
            vmem((2, LANES, NL), BF16), vmem((2, LANES, NL), BF16), vmem((2, 2, 64, NL), BF16),
            vmem((NL, LANES), F32), vmem((LANES, NL), F32), vmem((2, 64, NL), F32),
            vmem((BLOCK, NL), F32), vmem((BLOCK, NL), F32),
            vmem((NL, LANES), F32), vmem((NL, LANES), F32),
            vmem((2, ROWS, NL), F32), vmem((GROUP * ROWS, LANES), BF16), plane,
            vmem((8, BLOCK, LANES), BF16), vmem((8, BLOCK, LANES), BF16),
            vmem((BLOCK, LANES), BF16), vmem((8, ROWS, LANES), BF16),
            vmem((8, BLOCK, LANES), BF16), vmem((8, BLOCK, LANES), BF16),
            vmem((4, BLOCK, LANES), BF16), vmem((GROUP, ROWS, LANES), BF16),
            vmem((4, 2, ROWS, CHUNK), BF16), vmem((4, 2, ROWS, CHUNK), BF16),
            pltpu.SMEM((2,), F32), pltpu.SMEM((2,), F32),
            pltpu.SemaphoreType.DMA((7,)),
            pltpu.SemaphoreType.DMA((PHASES,)),
            pltpu.SemaphoreType.DMA((PHASES,)),
            pltpu.SemaphoreType.DMA((16,)),
        ],
        compiler_params=pltpu.CompilerParams(
            collective_id=0, has_side_effects=True, vmem_limit_bytes=60 * 2**20),
    )(source_field, receiver_field, line_inverse, lens_delay, omegas, image_weights)
    return fields[0], fields[1], gradient


def solution(mesh):
    placed = (
        P(None, "freq", "space", None),
        P(None, "freq", "space", None),
        P(None, "freq", None, None),
        P(None, "space", None),
        P("freq"),
        P("freq"),
    )
    return jax.shard_map(
        on_device,
        mesh=mesh,
        in_specs=placed,
        out_specs=(
            P(None, "freq", "space", None),
            P(None, "freq", "space", None),
            P(None, "space", None),
        ),
        check_vma=False,
    )
```

```python
import jax
import jax.numpy as jnp
from jax import lax
from jax.experimental import pallas as pl
from jax.experimental.pallas import tpu as pltpu
from jax.sharding import PartitionSpec as P

F32 = jnp.float32
BF16 = jnp.bfloat16
MESH = pl.DeviceIdType.MESH
LANES = 128
BLOCK = 32
NL = 1024
ROWS = 16
GROUP = 32
SHARDS = 64
CHUNK = 256
SWAP_SIGN = (-1.0, 1.0, 1.0, -1.0)

(A2A1, A2A2, A2A3, A2A4, LENS1, LENS2, FWD1, FWD2,
 SUM0, DIST0, SUM1, DIST1, PAIR, _, _, _, CROSS, _, _, _, HAND0, HAND1) = range(22)
PHASES = 22


def lanes(tile):
    return lax.broadcasted_iota(jnp.int32, tile.shape, 1)


def turn(tile, shift):
    return pltpu.roll(tile, shift % LANES, 1)


def even_block(tile):
    return (lanes(tile) // BLOCK) % 2 == 0


def block_transpose(tiles):
    t0, t1, t2, t3 = tiles
    low = lanes(t0) < 64
    even = even_block(t0)
    a0, a2 = jnp.where(low, t0, turn(t2, 64)), jnp.where(low, turn(t0, 64), t2)
    a1, a3 = jnp.where(low, t1, turn(t3, 64)), jnp.where(low, turn(t1, 64), t3)
    b0, b1 = jnp.where(even, a0, turn(a1, 32)), jnp.where(even, turn(a0, -32), a1)
    b2, b3 = jnp.where(even, a2, turn(a3, 32)), jnp.where(even, turn(a2, -32), a3)
    return b0, b1, b2, b3


def swap_parts(tile):
    return jnp.where(even_block(tile), turn(tile, -32), turn(tile, 32))


def outer_sign(tile):
    block = lanes(tile) // BLOCK
    return jnp.where((block == 0) | (block == 3), -1.0, 1.0)


def cos_sin(theta):
    n = jnp.floor(theta * 0.3183098861837907 + 0.5)
    r = theta - n * 3.140625
    r = r - n * 9.67502593994140625e-4
    r = r - n * 1.509957990978376e-7
    flip = 1.0 - 2.0 * (n - 2.0 * jnp.floor(n * 0.5))
    z = r * r
    s = -1.0 / 39916800.0
    for term in (1.0 / 362880.0, -1.0 / 5040.0, 1.0 / 120.0, -1.0 / 6.0, 1.0):
        s = s * z + term
    c = 1.0 / 479001600.0
    for term in (-1.0 / 3628800.0, 1.0 / 40320.0, -1.0 / 720.0, 1.0 / 24.0, -0.5, 1.0):
        c = c * z + term
    return c * flip, s * r * flip


def at(index, size):
    start = index * size
    return pl.ds(start if isinstance(start, int) else pl.multiple_of(start, size), size)


def kernel(src, rcv, minv, lens, om_hbm, wt_hbm, fields, grad,
           src_v, rcv_v, lens_v, m, mt, send1, got1, send2, got2, send3, got3, send4, got4,
           ya, yb, xa, xb, xf, acc_y, acc_x, acc_f, cos1, sin1, cos2, sin2, lens1, lens2_send, lens2,
           part0, sum0, dist0_send, dist0, part1, sum1, dist1_send, dist1,
           pair, cross, om, wt, load_sem, ss, rs, parts):
    src_out, rcv_out = fields.at[0], fields.at[1]
    fq = lax.axis_index("freq")
    s = lax.axis_index("space")
    h = s // GROUP
    k = lax.rem(s, GROUP)
    core = lax.rem(fq, 2)
    z_hi = fq // 2
    rank = 2 * fq + h
    mine = lax.rem(s, 2) == core

    def remote(source, target, phase, freq, space):
        return pltpu.make_async_remote_copy(
            src_ref=source, dst_ref=target, send_sem=ss.at[phase], recv_sem=rs.at[phase],
            device_id={"freq": freq, "space": space}, device_id_type=MESH)

    quarter = k // 8
    plane = s // 16

    def transposed(source, target, phase, part, space):
        pltpu.make_async_remote_copy(
            src_ref=source, dst_ref=target, send_sem=ss.at[phase], recv_sem=parts.at[4 * phase + part],
            device_id={"freq": fq, "space": space}, device_id_type=MESH).start()

    def wait_on(sem, ref):
        pltpu.make_async_copy(ref, ref, sem).wait()

    def give(source, target, phase, freq, space):
        here = (freq == fq) & (space == s)

        @pl.when(here)
        def _():
            pltpu.make_async_copy(source, target, rs.at[phase]).start()

        @pl.when(jnp.logical_not(here))
        def _():
            remote(source, target, phase, freq, space).start()

    loads = [
        pltpu.make_async_copy(src, src_v, load_sem.at[0]),
        pltpu.make_async_copy(rcv, rcv_v, load_sem.at[1]),
        pltpu.make_async_copy(lens, lens_v, load_sem.at[2]),
        pltpu.make_async_copy(om_hbm, om, load_sem.at[5]),
        pltpu.make_async_copy(wt_hbm, wt, load_sem.at[6]),
        pltpu.make_async_copy(minv.at[:, h], m.at[0], load_sem.at[3]),
        pltpu.make_async_copy(minv.at[:, 1 - h], m.at[1], load_sem.at[4]),
    ]
    for load in loads:
        load.start()
    barrier = pltpu.get_barrier_semaphore()
    pending = []
    own1 = (s == 0) | (s == SHARDS - 1)

    def sent(phase, ref, condition=None):
        def wait():
            if condition is None:
                wait_on(ss.at[phase], ref)
            else:
                pl.when(condition)(lambda: wait_on(ss.at[phase], ref))

        pending.append(wait)


    def greet(i, carry):
        pl.semaphore_signal(barrier, inc=1, device_id={"freq": fq, "space": lax.rem(s + i, SHARDS)},
                            device_id_type=MESH)
        return carry

    lax.fori_loop(1, SHARDS, greet, 0)
    for i in range(1, 4):
        pl.semaphore_signal(barrier, inc=1, device_id={"freq": lax.rem(fq + i, 4), "space": s},
                            device_id_type=MESH)
    for load in loads[:5]:
        load.wait()
    om_h = om[h]
    wt_h = wt[h]

    def rotate0(i, carry):
        f = i // 8
        q = lax.rem(i, 8)
        c, sn = cos_sin(om[f] * lens_v[0, :, at(q, LANES)])
        sre = src_v[0, f, :, at(q, LANES)].astype(F32)
        sim = src_v[1, f, :, at(q, LANES)].astype(F32)
        rre = rcv_v[0, f, :, at(q, LANES)].astype(F32)
        rim = rcv_v[1, f, :, at(q, LANES)].astype(F32)
        tiles = block_transpose((sre * c + sim * sn, sim * c - sre * sn,
                                 rre * c - rim * sn, rim * c + rre * sn))
        for p in range(4):
            send1[at(f * GROUP + 4 * q + p, ROWS), :] = tiles[p].astype(BF16)
        return carry

    lax.fori_loop(0, 16, rotate0, 0)
    got1[at(s, ROWS), :] = send1[at(s, ROWS), :]
    pl.semaphore_wait(barrier, SHARDS - 1 + 3)

    def send_all(send, got, phase, n):
        def one(i):
            t = n * 16 + lax.rem(s + i, 16)
            transposed(send.at[at(t, ROWS)], got.at[at(s, ROWS)], phase, plane, t)

        pl.when(n != plane)(lambda: one(0))
        for i in range(1, 16):
            one(i)

    def go1(i, carry):
        send_all(send1, got1, A2A1, lax.rem(plane + i, 4))
        return carry

    lax.fori_loop(0, 4, go1, 0)
    sent(A2A1, send1.at[pl.ds(0, ROWS * (SHARDS - 1))])

    @pl.when(mine)
    def _():
        for half in range(2):
            give(lens_v.at[1], lens1.at[core], LENS1, fq, half * GROUP + s // 2)

    sent(LENS1, lens_v.at[1], mine & own1)
    sent(LENS1, lens_v.at[pl.ds(0, 2)], mine & jnp.logical_not(own1))

    def pack2(q, carry):
        value = lens_v[2, :, at(q, LANES)]
        high = value.astype(BF16).astype(F32)
        rest = value - high
        middle = rest.astype(BF16).astype(F32)
        tiles = block_transpose((high, middle, rest - middle, jnp.zeros_like(value)))
        for p in range(4):
            lens2_send[at(4 * q + p, ROWS), :] = tiles[p].astype(BF16)
        return carry

    lax.fori_loop(0, 8, pack2, 0)

    def arrivals(phase, got, own, lines, use, last):
        for i in range(4):
            g = lax.rem(own + 4 - i, 4)
            wait_on(parts.at[4 * phase + g], got.at[pl.ds(0, CHUNK - (lines if i == 0 else 0))])
            if i < 3:
                use(g, i)
            else:
                last(g)

    def y_operands(got, other, g):
        for u in range(2):
            rows = at(2 * g + u, 128)
            tile = got[rows, :].astype(F32)
            other[rows, :] = (swap_parts(tile) * outer_sign(tile)).astype(BF16)

    def y_arrivals(phase, got, own, lines, start, finish):
        def part(g, rows):
            return (jnp.dot(m[0, 0, rows, at(g, CHUNK)], got[at(g, CHUNK), :], preferred_element_type=F32)
                    + jnp.dot(m[0, 1, rows, at(g, CHUNK)], ya[at(g, CHUNK), :], preferred_element_type=F32))

        def use(g, i):
            y_operands(got, ya, g)

            def body(n, carry):
                rows = at(n, CHUNK)
                acc_y[rows, :] = part(g, rows) if i == 0 else acc_y[rows, :] + part(g, rows)
                return carry

            lax.fori_loop(0, 4, body, 0)

        def last(g):
            y_operands(got, ya, g)

            def body(i, carry):
                n = lax.rem(start + i, 4)
                rows = at(n, CHUNK)
                finish(n, acc_y[rows, :] + part(g, rows))
                return carry

            lax.fori_loop(0, 4, body, 0)

        arrivals(phase, got, own, lines, use, last)

    def y_solve(first, second, n):
        rows = at(n, CHUNK)
        return (jnp.dot(m[0, 0, rows, :], first[...], preferred_element_type=F32)
                + jnp.dot(m[0, 1, rows, :], second[...], preferred_element_type=F32))

    def x_solve(f, first, second, n):
        columns = at(n, CHUNK)
        return (jnp.dot(first, mt[f, 0, :, columns], preferred_element_type=F32)
                + jnp.dot(second, mt[f, 1, :, columns], preferred_element_type=F32))

    def flip_matrix(f, begin, end):
        def body(i, carry):
            part = i // 8
            r = lax.rem(i, 8)
            mt[f, part, :, at(r, LANES)] = m[f, part, at(r, LANES), :].T
            return carry

        lax.fori_loop(begin, end, body, 0)

    def send_group(send, got, phase, n):
        def one(i):
            t = n * 8 + lax.rem(k + i, 8)
            transposed(send.at[at(t, BLOCK)], got.at[at(k, BLOCK)], phase, quarter, h * GROUP + t)

        pl.when(n != quarter)(lambda: one(0))
        for i in range(1, 8):
            one(i)

    loads[5].wait()
    flip_matrix(0, 0, 16)

    def finish1(n, new):
        send2[at(n, CHUNK), :] = new.astype(BF16)
        send_group(send2, got2, A2A2, n)

    y_arrivals(A2A1, got1, plane, ROWS, quarter, finish1)
    sent(A2A2, send2.at[pl.ds(0, BLOCK * (GROUP - 1))])
    got2[at(k, BLOCK), :] = send2[at(k, BLOCK), :]

    wait_on(rs.at[LENS1], lens1.at[0])
    forward1 = remote(lens1.at[core], lens1.at[core], FWD1, fq + 1 - 2 * core, s)
    forward1.start()
    pending.append(forward1.wait_send)

    skew = jnp.where(mine, 0, 1)

    def go_lens2(i):
        t = lax.rem(s + skew + 2 * i, SHARDS)
        remote(lens2_send.at[at(lax.rem(t, GROUP), ROWS)], lens2.at[at(s, ROWS)], LENS2, fq, t).start()

    pl.when(jnp.logical_not(mine))(lambda: go_lens2(0))
    for i in range(1, 32):
        go_lens2(i)
    sent(LENS2, lens2_send.at[pl.ds(0, ROWS * 31)], mine)
    sent(LENS2, lens2_send, jnp.logical_not(mine))

    @pl.when(mine)
    def _():
        lens2[at(s, ROWS), :] = lens2_send[at(k, ROWS), :]

    forward1.wait_recv()

    def trig1(q, carry):
        for b in range(2):
            c, sn = cos_sin(om_h * lens1[b, :, at(q, LANES)])
            cos1[pl.ds(b * ROWS, ROWS), at(q, LANES)] = c
            sin1[pl.ds(b * ROWS, ROWS), at(q, LANES)] = sn
        return carry

    lax.fori_loop(0, 8, trig1, 0)
    loads[6].wait()
    flip_matrix(1, 0, 8)

    def gather2(g):
        for u in range(2):
            q = 2 * g + u
            tiles = block_transpose([got2[at(4 * q + p, BLOCK), :].astype(F32) for p in range(4)])
            for c in range(4):
                xa[0, pl.ds(c * BLOCK, BLOCK), at(q, LANES)] = tiles[c].astype(BF16)
                xa[1, pl.ds(c * BLOCK, BLOCK), at(q, LANES)] = (SWAP_SIGN[c] * tiles[c ^ 1]).astype(BF16)

    def x_part(g, columns):
        return (jnp.dot(xa[0, :, at(g, CHUNK)], mt[0, 0, at(g, CHUNK), columns], preferred_element_type=F32)
                + jnp.dot(xa[1, :, at(g, CHUNK)], mt[0, 1, at(g, CHUNK), columns],
                          preferred_element_type=F32))

    def use2(g, i):
        gather2(g)

        def body(n, carry):
            columns = at(n, CHUNK)
            acc_x[:, columns] = x_part(g, columns) if i == 0 else acc_x[:, columns] + x_part(g, columns)
            return carry

        lax.fori_loop(0, 4, body, 0)

    def last2(g):
        gather2(g)

        def body(n, carry):
            solve2(n, acc_x[:, at(n, CHUNK)] + x_part(g, at(n, CHUNK)))
            return carry

        lax.fori_loop(0, 4, body, 0)

    def solve2(n, new):
        sre, sim, rre, rim = (new[c * BLOCK:(c + 1) * BLOCK] for c in range(4))
        image = wt_h * (sre * rre + sim * rim)
        for u in range(2):
            part0[2 * n + u] = image[:, u * LANES:(u + 1) * LANES].astype(BF16)
        c, sn = cos1[:, at(n, CHUNK)], sin1[:, at(n, CHUNK)]
        turned = (sre * c + sim * sn, sim * c - sre * sn, rre * c - rim * sn, rim * c + rre * sn)
        for part in range(4):
            xb[0, pl.ds(part * BLOCK, BLOCK), at(n, CHUNK)] = turned[part].astype(BF16)
            xb[1, pl.ds(part * BLOCK, BLOCK), at(n, CHUNK)] = (
                SWAP_SIGN[part] * turned[part ^ 1]).astype(BF16)

    arrivals(A2A2, got2, quarter, BLOCK, use2, last2)

    def solve3(i, carry):
        n = lax.rem(k // 8 + i, 4)
        new = x_solve(0, xb[0], xb[1], n)
        for u in range(2):
            tiles = block_transpose([new[c * BLOCK:(c + 1) * BLOCK, u * LANES:(u + 1) * LANES]
                                     for c in range(4)])
            for p in range(4):
                send3[at(8 * n + 4 * u + p, BLOCK), :] = tiles[p].astype(BF16)
        send_group(send3, got3, A2A3, n)
        return carry

    lax.fori_loop(0, 4, solve3, 0)
    sent(A2A3, send3.at[pl.ds(0, BLOCK * (GROUP - 1))])
    got3[at(k, BLOCK), :] = send3[at(k, BLOCK), :]

    def sum_send(part, total, phase):
        total[rank] = part[rank]

        def body(i, carry):
            j = lax.rem(rank + i, 8)
            remote(part.at[j], total.at[rank], phase, j // 2, lax.rem(j, 2) * GROUP + k).start()
            return carry

        lax.fori_loop(1, 8, body, 0)
        sent(phase, part.at[pl.ds(0, 7)])

    def sum_up(total, phase):
        wait_on(rs.at[phase], total.at[pl.ds(0, 7)])
        value = total[0].astype(F32)
        for j in range(1, 8):
            value += total[j].astype(F32)
        return value

    sum_send(part0, sum0, SUM0)

    forward2 = remote(lens2, lens2, FWD2, fq + 1 - 2 * core, s)

    @pl.when(mine)
    def _():
        wait_on(rs.at[LENS2], lens2.at[pl.ds(0, ROWS * (SHARDS - 1))])
        forward2.start()

    @pl.when(jnp.logical_not(mine))
    def _():
        forward2.wait_recv()

    sent(FWD2, lens2, mine)

    def trig2(i, carry):
        terms = lens2[at(i, 128), :].astype(F32)
        value = (terms + turn(terms, -32)) + turn(terms, -64)
        value = jnp.where(lanes(value) < BLOCK, value, 0.0)
        value = value + turn(value, 32)
        value = value + turn(value, 64)
        c, sn = cos_sin(om_h * value)
        cos2[at(i, 128), :] = c
        sin2[at(i, 128), :] = -outer_sign(sn) * sn
        return carry

    lax.fori_loop(0, 8, trig2, 0)
    flip_matrix(1, 8, 16)

    def solve4(n, new):
        product = wt_h * new * turn(new, 64)
        image = product + turn(product, -32)
        for u in range(2):
            packed = image[u * 128:u * 128 + BLOCK]
            block = lanes(packed) // BLOCK
            for a in range(1, 4):
                rows = image[u * 128 + a * BLOCK:u * 128 + (a + 1) * BLOCK]
                packed = jnp.where(block == a, turn(rows, a * BLOCK), packed)
            part1[2 * n + u] = packed.astype(BF16)
        turned = new * cos2[at(n, CHUNK), :] + swap_parts(new) * sin2[at(n, CHUNK), :]
        yb[0, at(n, CHUNK), :] = turned.astype(BF16)
        yb[1, at(n, CHUNK), :] = (swap_parts(turned) * outer_sign(turned)).astype(BF16)

    y_arrivals(A2A3, got3, quarter, BLOCK, 0, solve4)
    sum_send(part1, sum1, SUM1)

    def solve5(i, carry):
        n = lax.rem(plane + i, 4)
        send4[at(n, CHUNK), :] = y_solve(yb.at[0], yb.at[1], n).astype(BF16)

        send_all(send4, got4, A2A4, n)
        return carry

    lax.fori_loop(0, 4, solve5, 0)
    sent(A2A4, send4.at[pl.ds(0, ROWS * (SHARDS - 1))])
    got4[at(s, ROWS), :] = send4[at(s, ROWS), :]

    dist0_send[...] = sum_up(sum0, SUM0).astype(BF16)
    for up in range(2):
        for b in range(2):
            give(dist0_send.at[pl.ds(b * ROWS, ROWS)], dist0.at[h, fq], DIST0, 2 * up + h, 2 * k + b)
    sent(DIST0, dist0.at[0, pl.ds(0, 3)], own1 & (core == h))
    sent(DIST0, dist0.at[0], jnp.logical_not(own1 & (core == h)))

    total1 = sum_up(sum1, SUM1)
    for d in range(4):
        dist1_send[d] = turn(total1, d * BLOCK).astype(BF16)

    side = lax.rem(k, 2)

    def dist1_copy(i):
        d = lax.rem(k + 4 - i // 2, 4)
        return dist1_send.at[d, at(i % 2, ROWS)], dist1.at[side, k // 2], DIST1

    for i in range(8):
        remote(*dist1_copy(i), side + 2 * (1 - z_hi), 8 * rank + i).start()
    for i in range(8):
        give(*dist1_copy(i), side + 2 * z_hi, 8 * rank + i)
    own_dist = (s // 8 == rank) & (core == side)
    sent(DIST1, dist1.at[0, pl.ds(0, 15)], own_dist)
    sent(DIST1, dist1.at[0], jnp.logical_not(own_dist))

    acc_f[...] = jnp.zeros_like(acc_f)

    def gather4(g):
        f = g // 2
        for u in range(4):
            q = 4 * lax.rem(g, 2) + u
            tiles = block_transpose([got4[at(f * GROUP + 4 * q + p, ROWS), :].astype(F32) for p in range(4)])
            for c in range(4):
                xf[f, 0, pl.ds(c * ROWS, ROWS), at(q, LANES)] = tiles[c].astype(BF16)
                xf[f, 1, pl.ds(c * ROWS, ROWS), at(q, LANES)] = (SWAP_SIGN[c] * tiles[c ^ 1]).astype(BF16)

    def f_part(g, columns):
        f = g // 2
        which = jnp.where(h == f, 0, 1)
        terms = at(lax.rem(g, 2), 512)
        return (jnp.dot(xf[f, 0, :, terms], mt[which, 0, terms, columns], preferred_element_type=F32)
                + jnp.dot(xf[f, 1, :, terms], mt[which, 1, terms, columns], preferred_element_type=F32))

    def use4(g, i):
        gather4(g)

        def body(n, carry):
            acc_f[g // 2, :, at(n, CHUNK)] += f_part(g, at(n, CHUNK))
            return carry

        lax.fori_loop(0, 4, body, 0)

    def pair_copy(n):
        return remote(pair.at[n, core], pair.at[n, core], PAIR + n, fq + 1 - 2 * core, s)

    def cross_copy(n):
        return remote(cross.at[n, z_hi], cross.at[n, z_hi], CROSS + n, lax.rem(fq + 2, 4), s)

    def pass_on(n):
        pair_copy(n).wait_recv()
        cross[n, z_hi] = (pair[n, 0].astype(F32) + pair[n, 1].astype(F32)).astype(BF16)
        cross_copy(n).start()
        pending.append(pair_copy(n).wait_send)
        pending.append(cross_copy(n).wait_send)

    def last4(g):
        gather4(g)
        for n in range(4):
            image = jnp.zeros((ROWS, CHUNK), F32)
            for u in range(2):
                f = g // 2 if u == 0 else 1 - g // 2
                new = acc_f[f, :, at(n, CHUNK)]
                if u == 0:
                    new += f_part(g, at(n, CHUNK))
                sre, sim, rre, rim = (new[c * ROWS:(c + 1) * ROWS] for c in range(4))
                src_out[0, f, :, at(n, CHUNK)] = sre.astype(BF16)
                src_out[1, f, :, at(n, CHUNK)] = sim.astype(BF16)
                rcv_out[0, f, :, at(n, CHUNK)] = rre.astype(BF16)
                rcv_out[1, f, :, at(n, CHUNK)] = rim.astype(BF16)
                image += wt[f] * (sre * rre + sim * rim)
            pair[n, core] = image.astype(BF16)
            pair_copy(n).start()
            if n > 0:
                pass_on(n - 1)
        pass_on(3)

    arrivals(A2A4, got4, plane, ROWS, use4, last4)

    wait_on(rs.at[DIST0], dist0.at[0])
    wait_on(rs.at[DIST1], dist1.at[0])
    hands = [remote(dist0.at[core], dist0.at[core], HAND0, fq + 1 - 2 * core, s),
             remote(dist1.at[core], dist1.at[core], HAND1, fq + 1 - 2 * core, s)]
    for hand in hands:
        hand.start()
        pending.append(hand.wait_send)
    for hand in hands:
        hand.wait_recv()
    for j in range(8):
        grad[0, :, pl.ds(j * LANES, LANES)] = dist0[j % 2, j // 2].astype(F32)
        tile = dist1[0, 2 * j].astype(F32)
        block = lanes(tile) // BLOCK
        for p in range(1, 4):
            tile = jnp.where(block == p, dist1[p % 2, 2 * j + p // 2].astype(F32), tile)
        grad[1, :, pl.ds(j * LANES, LANES)] = tile

    for wait in pending:
        wait()

    for n in range(4):
        cross_copy(n).wait_recv()
        grad[2, :, at(n, CHUNK)] = cross[n, 0].astype(F32) + cross[n, 1].astype(F32)


def on_device(source_field, receiver_field, line_inverse, lens_delay, omegas, image_weights):
    vmem = pltpu.VMEM
    plane = vmem((NL, LANES), BF16)
    fields, gradient = pl.pallas_call(
        kernel,
        out_shape=(
            vmem((2,) + source_field.shape, BF16),
            vmem(lens_delay.shape, F32),
        ),
        in_specs=[pl.BlockSpec(memory_space=pl.ANY)] * 6,
        out_specs=[pl.BlockSpec(memory_space=vmem)] * 2,
        scratch_shapes=[
            vmem(source_field.shape, BF16), vmem(receiver_field.shape, BF16), vmem(lens_delay.shape, F32),
            vmem((2, 2, NL, NL), BF16), vmem((2, 2, NL, NL), BF16),
            plane, plane, plane, plane, plane, plane, plane, plane,
            plane, vmem((2, NL, LANES), BF16),
            vmem((2, LANES, NL), BF16), vmem((2, LANES, NL), BF16), vmem((2, 2, 64, NL), BF16),
            vmem((NL, LANES), F32), vmem((LANES, NL), F32), vmem((2, 64, NL), F32),
            vmem((BLOCK, NL), F32), vmem((BLOCK, NL), F32),
            vmem((NL, LANES), F32), vmem((NL, LANES), F32),
            vmem((2, ROWS, NL), F32), vmem((GROUP * ROWS, LANES), BF16), plane,
            vmem((8, BLOCK, LANES), BF16), vmem((8, BLOCK, LANES), BF16),
            vmem((BLOCK, LANES), BF16), vmem((2, 4, ROWS, LANES), BF16),
            vmem((8, BLOCK, LANES), BF16), vmem((8, BLOCK, LANES), BF16),
            vmem((4, BLOCK, LANES), BF16), vmem((2, GROUP // 2, ROWS, LANES), BF16),
            vmem((4, 2, ROWS, CHUNK), BF16), vmem((4, 2, ROWS, CHUNK), BF16),
            pltpu.SMEM((2,), F32), pltpu.SMEM((2,), F32),
            pltpu.SemaphoreType.DMA((7,)),
            pltpu.SemaphoreType.DMA((PHASES,)),
            pltpu.SemaphoreType.DMA((PHASES,)),
            pltpu.SemaphoreType.DMA((16,)),
        ],
        compiler_params=pltpu.CompilerParams(
            collective_id=0, has_side_effects=True, vmem_limit_bytes=60 * 2**20),
    )(source_field, receiver_field, line_inverse, lens_delay, omegas, image_weights)
    return fields[0], fields[1], gradient


def solution(mesh):
    placed = (
        P(None, "freq", "space", None),
        P(None, "freq", "space", None),
        P(None, "freq", None, None),
        P(None, "space", None),
        P("freq"),
        P("freq"),
    )
    return jax.shard_map(
        on_device,
        mesh=mesh,
        in_specs=placed,
        out_specs=(
            P(None, "freq", "space", None),
            P(None, "freq", "space", None),
            P(None, "space", None),
        ),
        check_vma=False,
    )
```

```python
import jax
import jax.numpy as jnp
from jax import lax
from jax.experimental import pallas as pl
from jax.experimental.pallas import tpu as pltpu
from jax.sharding import PartitionSpec as P

F32 = jnp.float32
BF16 = jnp.bfloat16
MESH = pl.DeviceIdType.MESH
LANES = 128
BLOCK = 32
NL = 1024
ROWS = 16
GROUP = 32
SHARDS = 64
CHUNK = 256
SWAP_SIGN = (-1.0, 1.0, 1.0, -1.0)

(A2A1, A2A2, A2A3, A2A4, LENS1, LENS2, FWD1, FWD2,
 SUM0, DIST0, SUM1, DIST1, PAIR, _, _, _, CROSS, _, _, _, HAND0, HAND1) = range(22)
PHASES = 22


def lanes(tile):
    return lax.broadcasted_iota(jnp.int32, tile.shape, 1)


def turn(tile, shift):
    return pltpu.roll(tile, shift % LANES, 1)


def even_block(tile):
    return (lanes(tile) // BLOCK) % 2 == 0


def block_transpose(tiles):
    t0, t1, t2, t3 = tiles
    low = lanes(t0) < 64
    even = even_block(t0)
    a0, a2 = jnp.where(low, t0, turn(t2, 64)), jnp.where(low, turn(t0, 64), t2)
    a1, a3 = jnp.where(low, t1, turn(t3, 64)), jnp.where(low, turn(t1, 64), t3)
    b0, b1 = jnp.where(even, a0, turn(a1, 32)), jnp.where(even, turn(a0, -32), a1)
    b2, b3 = jnp.where(even, a2, turn(a3, 32)), jnp.where(even, turn(a2, -32), a3)
    return b0, b1, b2, b3


def swap_parts(tile):
    return jnp.where(even_block(tile), turn(tile, -32), turn(tile, 32))


def outer_sign(tile):
    block = lanes(tile) // BLOCK
    return jnp.where((block == 0) | (block == 3), -1.0, 1.0)


def cos_sin(theta):
    n = jnp.floor(theta * 0.3183098861837907 + 0.5)
    r = theta - n * 3.140625
    r = r - n * 9.67502593994140625e-4
    r = r - n * 1.509957990978376e-7
    flip = 1.0 - 2.0 * (n - 2.0 * jnp.floor(n * 0.5))
    z = r * r
    s = -1.0 / 39916800.0
    for term in (1.0 / 362880.0, -1.0 / 5040.0, 1.0 / 120.0, -1.0 / 6.0, 1.0):
        s = s * z + term
    c = 1.0 / 479001600.0
    for term in (-1.0 / 3628800.0, 1.0 / 40320.0, -1.0 / 720.0, 1.0 / 24.0, -0.5, 1.0):
        c = c * z + term
    return c * flip, s * r * flip


def at(index, size):
    start = index * size
    return pl.ds(start if isinstance(start, int) else pl.multiple_of(start, size), size)


def kernel(src, rcv, minv, lens, om_hbm, wt_hbm, fields, grad,
           src_v, rcv_v, lens_v, m, mt, send1, got1, send2, got2, send3, got3, send4, got4,
           ya, yb, xa, xb, xf, acc_y, acc_x, acc_f, cos1, sin1, cos2, sin2, lens1, lens2_send, lens2,
           part0, sum0, dist0_send, dist0, part1, sum1, dist1_send, dist1,
           pair, cross, om, wt, load_sem, ss, rs, parts):
    src_out, rcv_out = fields.at[0], fields.at[1]
    fq = lax.axis_index("freq")
    s = lax.axis_index("space")
    h = s // GROUP
    k = lax.rem(s, GROUP)
    core = lax.rem(fq, 2)
    z_hi = fq // 2
    rank = 2 * fq + h
    mine = lax.rem(s, 2) == core

    def remote(source, target, phase, freq, space):
        return pltpu.make_async_remote_copy(
            src_ref=source, dst_ref=target, send_sem=ss.at[phase], recv_sem=rs.at[phase],
            device_id={"freq": freq, "space": space}, device_id_type=MESH)

    quarter = k // 8
    plane = s // 16

    def transposed(source, target, phase, part, space):
        pltpu.make_async_remote_copy(
            src_ref=source, dst_ref=target, send_sem=ss.at[phase], recv_sem=parts.at[4 * phase + part],
            device_id={"freq": fq, "space": space}, device_id_type=MESH).start()

    def wait_on(sem, ref):
        pltpu.make_async_copy(ref, ref, sem).wait()

    def give(source, target, phase, freq, space):
        here = (freq == fq) & (space == s)

        @pl.when(here)
        def _():
            pltpu.make_async_copy(source, target, rs.at[phase]).start()

        @pl.when(jnp.logical_not(here))
        def _():
            remote(source, target, phase, freq, space).start()

    loads = [
        pltpu.make_async_copy(src, src_v, load_sem.at[0]),
        pltpu.make_async_copy(rcv, rcv_v, load_sem.at[1]),
        pltpu.make_async_copy(lens, lens_v, load_sem.at[2]),
        pltpu.make_async_copy(om_hbm, om, load_sem.at[5]),
        pltpu.make_async_copy(wt_hbm, wt, load_sem.at[6]),
        pltpu.make_async_copy(minv.at[:, h], m.at[0], load_sem.at[3]),
        pltpu.make_async_copy(minv.at[:, 1 - h], m.at[1], load_sem.at[4]),
    ]
    for load in loads:
        load.start()
    barrier = pltpu.get_barrier_semaphore()
    pending = []
    own1 = (s == 0) | (s == SHARDS - 1)

    def sent(phase, ref, condition=None):
        def wait():
            if condition is None:
                wait_on(ss.at[phase], ref)
            else:
                pl.when(condition)(lambda: wait_on(ss.at[phase], ref))

        pending.append(wait)


    def greet(i, carry):
        pl.semaphore_signal(barrier, inc=1, device_id={"freq": fq, "space": lax.rem(s + i, SHARDS)},
                            device_id_type=MESH)
        return carry

    lax.fori_loop(1, SHARDS, greet, 0)
    for i in range(1, 4):
        pl.semaphore_signal(barrier, inc=1, device_id={"freq": lax.rem(fq + i, 4), "space": s},
                            device_id_type=MESH)
    for load in loads[:5]:
        load.wait()
    om_h = om[h]
    wt_h = wt[h]

    def rotate0(i, carry):
        f = i // 8
        q = lax.rem(i, 8)
        c, sn = cos_sin(om[f] * lens_v[0, :, at(q, LANES)])
        sre = src_v[0, f, :, at(q, LANES)].astype(F32)
        sim = src_v[1, f, :, at(q, LANES)].astype(F32)
        rre = rcv_v[0, f, :, at(q, LANES)].astype(F32)
        rim = rcv_v[1, f, :, at(q, LANES)].astype(F32)
        tiles = block_transpose((sre * c + sim * sn, sim * c - sre * sn,
                                 rre * c - rim * sn, rim * c + rre * sn))
        for p in range(4):
            send1[at(f * GROUP + 4 * q + p, ROWS), :] = tiles[p].astype(BF16)
        return carry

    lax.fori_loop(0, 16, rotate0, 0)
    got1[at(s, ROWS), :] = send1[at(s, ROWS), :]
    pl.semaphore_wait(barrier, SHARDS - 1 + 3)

    def send_all(send, got, phase, n):
        def one(i):
            t = n * 16 + lax.rem(s + i, 16)
            transposed(send.at[at(t, ROWS)], got.at[at(s, ROWS)], phase, plane, t)

        pl.when(n != plane)(lambda: one(0))
        for i in range(1, 16):
            one(i)

    def go1(i, carry):
        send_all(send1, got1, A2A1, lax.rem(plane + i, 4))
        return carry

    lax.fori_loop(0, 4, go1, 0)
    sent(A2A1, send1.at[pl.ds(0, ROWS * (SHARDS - 1))])

    @pl.when(mine)
    def _():
        for half in range(2):
            give(lens_v.at[1], lens1.at[core], LENS1, fq, half * GROUP + s // 2)

    sent(LENS1, lens_v.at[1], mine & own1)
    sent(LENS1, lens_v.at[pl.ds(0, 2)], mine & jnp.logical_not(own1))

    def pack2(q, carry):
        value = lens_v[2, :, at(q, LANES)]
        high = value.astype(BF16).astype(F32)
        rest = value - high
        middle = rest.astype(BF16).astype(F32)
        tiles = block_transpose((high, middle, rest - middle, jnp.zeros_like(value)))
        for p in range(4):
            lens2_send[at(4 * q + p, ROWS), :] = tiles[p].astype(BF16)
        return carry

    lax.fori_loop(0, 8, pack2, 0)

    def arrivals(phase, got, own, lines, use, last):
        for i in range(4):
            g = lax.rem(own + 4 - i, 4)
            wait_on(parts.at[4 * phase + g], got.at[pl.ds(0, CHUNK - (lines if i == 0 else 0))])
            if i < 3:
                use(g, i)
            else:
                last(g)

    def y_operands(got, other, g):
        for u in range(2):
            rows = at(2 * g + u, 128)
            tile = got[rows, :].astype(F32)
            other[rows, :] = (swap_parts(tile) * outer_sign(tile)).astype(BF16)

    def y_arrivals(phase, got, own, lines, start, finish):
        def part(g, rows):
            return (jnp.dot(m[0, 0, rows, at(g, CHUNK)], got[at(g, CHUNK), :], preferred_element_type=F32)
                    + jnp.dot(m[0, 1, rows, at(g, CHUNK)], ya[at(g, CHUNK), :], preferred_element_type=F32))

        def use(g, i):
            y_operands(got, ya, g)

            def body(n, carry):
                rows = at(n, CHUNK)
                acc_y[rows, :] = part(g, rows) if i == 0 else acc_y[rows, :] + part(g, rows)
                return carry

            lax.fori_loop(0, 4, body, 0)

        def last(g):
            y_operands(got, ya, g)

            def body(i, carry):
                n = lax.rem(start + i, 4)
                rows = at(n, CHUNK)
                finish(n, acc_y[rows, :] + part(g, rows))
                return carry

            lax.fori_loop(0, 4, body, 0)

        arrivals(phase, got, own, lines, use, last)

    def y_solve(first, second, n):
        rows = at(n, CHUNK)
        return (jnp.dot(m[0, 0, rows, :], first[...], preferred_element_type=F32)
                + jnp.dot(m[0, 1, rows, :], second[...], preferred_element_type=F32))

    def x_solve(f, first, second, n):
        columns = at(n, CHUNK)
        return (jnp.dot(first, mt[f, 0, :, columns], preferred_element_type=F32)
                + jnp.dot(second, mt[f, 1, :, columns], preferred_element_type=F32))

    def flip_matrix(f, begin, end):
        def body(i, carry):
            part = i // 8
            r = lax.rem(i, 8)
            mt[f, part, :, at(r, LANES)] = m[f, part, at(r, LANES), :].T
            return carry

        lax.fori_loop(begin, end, body, 0)

    def send_group(send, got, phase, n):
        def one(i):
            t = n * 8 + lax.rem(k + i, 8)
            transposed(send.at[at(t, BLOCK)], got.at[at(k, BLOCK)], phase, quarter, h * GROUP + t)

        pl.when(n != quarter)(lambda: one(0))
        for i in range(1, 8):
            one(i)

    loads[5].wait()
    flip_matrix(0, 0, 16)
    loads[6].wait()
    flip_matrix(1, 0, 16)

    def finish1(n, new):
        send2[at(n, CHUNK), :] = new.astype(BF16)
        send_group(send2, got2, A2A2, n)

    y_arrivals(A2A1, got1, plane, ROWS, quarter, finish1)
    sent(A2A2, send2.at[pl.ds(0, BLOCK * (GROUP - 1))])
    got2[at(k, BLOCK), :] = send2[at(k, BLOCK), :]

    wait_on(rs.at[LENS1], lens1.at[0])
    forward1 = remote(lens1.at[core], lens1.at[core], FWD1, fq + 1 - 2 * core, s)
    forward1.start()
    pending.append(forward1.wait_send)

    skew = jnp.where(mine, 0, 1)

    def go_lens2(i):
        t = lax.rem(s + skew + 2 * i, SHARDS)
        remote(lens2_send.at[at(lax.rem(t, GROUP), ROWS)], lens2.at[at(s, ROWS)], LENS2, fq, t).start()

    pl.when(jnp.logical_not(mine))(lambda: go_lens2(0))
    for i in range(1, 32):
        go_lens2(i)
    sent(LENS2, lens2_send.at[pl.ds(0, ROWS * 31)], mine)
    sent(LENS2, lens2_send, jnp.logical_not(mine))

    @pl.when(mine)
    def _():
        lens2[at(s, ROWS), :] = lens2_send[at(k, ROWS), :]

    forward1.wait_recv()

    def trig1(q, carry):
        for b in range(2):
            c, sn = cos_sin(om_h * lens1[b, :, at(q, LANES)])
            cos1[pl.ds(b * ROWS, ROWS), at(q, LANES)] = c
            sin1[pl.ds(b * ROWS, ROWS), at(q, LANES)] = sn
        return carry

    lax.fori_loop(0, 8, trig1, 0)

    def gather2(g):
        for u in range(2):
            q = 2 * g + u
            tiles = block_transpose([got2[at(4 * q + p, BLOCK), :].astype(F32) for p in range(4)])
            for c in range(4):
                xa[0, pl.ds(c * BLOCK, BLOCK), at(q, LANES)] = tiles[c].astype(BF16)
                xa[1, pl.ds(c * BLOCK, BLOCK), at(q, LANES)] = (SWAP_SIGN[c] * tiles[c ^ 1]).astype(BF16)

    def x_part(g, columns):
        return (jnp.dot(xa[0, :, at(g, CHUNK)], mt[0, 0, at(g, CHUNK), columns], preferred_element_type=F32)
                + jnp.dot(xa[1, :, at(g, CHUNK)], mt[0, 1, at(g, CHUNK), columns],
                          preferred_element_type=F32))

    def use2(g, i):
        gather2(g)

        def body(n, carry):
            columns = at(n, CHUNK)
            acc_x[:, columns] = x_part(g, columns) if i == 0 else acc_x[:, columns] + x_part(g, columns)
            return carry

        lax.fori_loop(0, 4, body, 0)

    def last2(g):
        gather2(g)

        def body(n, carry):
            solve2(n, acc_x[:, at(n, CHUNK)] + x_part(g, at(n, CHUNK)))
            return carry

        lax.fori_loop(0, 4, body, 0)

    def solve2(n, new):
        sre, sim, rre, rim = (new[c * BLOCK:(c + 1) * BLOCK] for c in range(4))
        image = wt_h * (sre * rre + sim * rim)
        for u in range(2):
            part0[2 * n + u] = image[:, u * LANES:(u + 1) * LANES].astype(BF16)
        c, sn = cos1[:, at(n, CHUNK)], sin1[:, at(n, CHUNK)]
        turned = (sre * c + sim * sn, sim * c - sre * sn, rre * c - rim * sn, rim * c + rre * sn)
        for part in range(4):
            xb[0, pl.ds(part * BLOCK, BLOCK), at(n, CHUNK)] = turned[part].astype(BF16)
            xb[1, pl.ds(part * BLOCK, BLOCK), at(n, CHUNK)] = (
                SWAP_SIGN[part] * turned[part ^ 1]).astype(BF16)

    arrivals(A2A2, got2, quarter, BLOCK, use2, last2)

    def solve3(i, carry):
        n = lax.rem(k // 8 + i, 4)
        new = x_solve(0, xb[0], xb[1], n)
        for u in range(2):
            tiles = block_transpose([new[c * BLOCK:(c + 1) * BLOCK, u * LANES:(u + 1) * LANES]
                                     for c in range(4)])
            for p in range(4):
                send3[at(8 * n + 4 * u + p, BLOCK), :] = tiles[p].astype(BF16)
        send_group(send3, got3, A2A3, n)
        return carry

    lax.fori_loop(0, 4, solve3, 0)
    sent(A2A3, send3.at[pl.ds(0, BLOCK * (GROUP - 1))])
    got3[at(k, BLOCK), :] = send3[at(k, BLOCK), :]

    def sum_send(part, total, phase):
        total[rank] = part[rank]

        def body(i, carry):
            j = lax.rem(rank + i, 8)
            remote(part.at[j], total.at[rank], phase, j // 2, lax.rem(j, 2) * GROUP + k).start()
            return carry

        lax.fori_loop(1, 8, body, 0)
        sent(phase, part.at[pl.ds(0, 7)])

    def sum_up(total, phase):
        wait_on(rs.at[phase], total.at[pl.ds(0, 7)])
        value = total[0].astype(F32)
        for j in range(1, 8):
            value += total[j].astype(F32)
        return value

    sum_send(part0, sum0, SUM0)

    forward2 = remote(lens2, lens2, FWD2, fq + 1 - 2 * core, s)

    @pl.when(mine)
    def _():
        wait_on(rs.at[LENS2], lens2.at[pl.ds(0, ROWS * (SHARDS - 1))])
        forward2.start()

    @pl.when(jnp.logical_not(mine))
    def _():
        forward2.wait_recv()

    sent(FWD2, lens2, mine)

    def trig2(i, carry):
        terms = lens2[at(i, 128), :].astype(F32)
        value = (terms + turn(terms, -32)) + turn(terms, -64)
        value = jnp.where(lanes(value) < BLOCK, value, 0.0)
        value = value + turn(value, 32)
        value = value + turn(value, 64)
        c, sn = cos_sin(om_h * value)
        cos2[at(i, 128), :] = c
        sin2[at(i, 128), :] = -outer_sign(sn) * sn
        return carry

    lax.fori_loop(0, 8, trig2, 0)

    def solve4(n, new):
        product = wt_h * new * turn(new, 64)
        image = product + turn(product, -32)
        for u in range(2):
            packed = image[u * 128:u * 128 + BLOCK]
            block = lanes(packed) // BLOCK
            for a in range(1, 4):
                rows = image[u * 128 + a * BLOCK:u * 128 + (a + 1) * BLOCK]
                packed = jnp.where(block == a, turn(rows, a * BLOCK), packed)
            part1[2 * n + u] = packed.astype(BF16)
        turned = new * cos2[at(n, CHUNK), :] + swap_parts(new) * sin2[at(n, CHUNK), :]
        yb[0, at(n, CHUNK), :] = turned.astype(BF16)
        yb[1, at(n, CHUNK), :] = (swap_parts(turned) * outer_sign(turned)).astype(BF16)

    y_arrivals(A2A3, got3, quarter, BLOCK, 0, solve4)
    sum_send(part1, sum1, SUM1)

    def solve5(i, carry):
        n = lax.rem(plane + i, 4)
        send4[at(n, CHUNK), :] = y_solve(yb.at[0], yb.at[1], n).astype(BF16)

        send_all(send4, got4, A2A4, n)
        return carry

    lax.fori_loop(0, 4, solve5, 0)
    sent(A2A4, send4.at[pl.ds(0, ROWS * (SHARDS - 1))])
    got4[at(s, ROWS), :] = send4[at(s, ROWS), :]

    dist0_send[...] = sum_up(sum0, SUM0).astype(BF16)
    for up in range(2):
        for b in range(2):
            give(dist0_send.at[pl.ds(b * ROWS, ROWS)], dist0.at[h, fq], DIST0, 2 * up + h, 2 * k + b)
    sent(DIST0, dist0.at[0, pl.ds(0, 3)], own1 & (core == h))
    sent(DIST0, dist0.at[0], jnp.logical_not(own1 & (core == h)))

    total1 = sum_up(sum1, SUM1)
    for d in range(4):
        dist1_send[d] = turn(total1, d * BLOCK).astype(BF16)

    side = lax.rem(k, 2)

    def dist1_copy(i):
        d = lax.rem(k + 4 - i // 2, 4)
        return dist1_send.at[d, at(i % 2, ROWS)], dist1.at[side, k // 2], DIST1

    for i in range(8):
        remote(*dist1_copy(i), side + 2 * (1 - z_hi), 8 * rank + i).start()
    for i in range(8):
        give(*dist1_copy(i), side + 2 * z_hi, 8 * rank + i)
    own_dist = (s // 8 == rank) & (core == side)
    sent(DIST1, dist1.at[0, pl.ds(0, 15)], own_dist)
    sent(DIST1, dist1.at[0], jnp.logical_not(own_dist))

    acc_f[...] = jnp.zeros_like(acc_f)

    def gather4(g):
        f = g // 2
        for u in range(4):
            q = 4 * lax.rem(g, 2) + u
            tiles = block_transpose([got4[at(f * GROUP + 4 * q + p, ROWS), :].astype(F32) for p in range(4)])
            for c in range(4):
                xf[f, 0, pl.ds(c * ROWS, ROWS), at(q, LANES)] = tiles[c].astype(BF16)
                xf[f, 1, pl.ds(c * ROWS, ROWS), at(q, LANES)] = (SWAP_SIGN[c] * tiles[c ^ 1]).astype(BF16)

    def f_part(g, columns):
        f = g // 2
        which = jnp.where(h == f, 0, 1)
        terms = at(lax.rem(g, 2), 512)
        return (jnp.dot(xf[f, 0, :, terms], mt[which, 0, terms, columns], preferred_element_type=F32)
                + jnp.dot(xf[f, 1, :, terms], mt[which, 1, terms, columns], preferred_element_type=F32))

    def use4(g, i):
        gather4(g)

        def body(n, carry):
            acc_f[g // 2, :, at(n, CHUNK)] += f_part(g, at(n, CHUNK))
            return carry

        lax.fori_loop(0, 4, body, 0)

    def pair_copy(n):
        return remote(pair.at[n, core], pair.at[n, core], PAIR + n, fq + 1 - 2 * core, s)

    def cross_copy(n):
        return remote(cross.at[n, z_hi], cross.at[n, z_hi], CROSS + n, lax.rem(fq + 2, 4), s)

    def pass_on(n):
        pair_copy(n).wait_recv()
        cross[n, z_hi] = (pair[n, 0].astype(F32) + pair[n, 1].astype(F32)).astype(BF16)
        cross_copy(n).start()
        pending.append(pair_copy(n).wait_send)
        pending.append(cross_copy(n).wait_send)

    def last4(g):
        gather4(g)
        for n in range(4):
            image = jnp.zeros((ROWS, CHUNK), F32)
            for u in range(2):
                f = g // 2 if u == 0 else 1 - g // 2
                new = acc_f[f, :, at(n, CHUNK)]
                if u == 0:
                    new += f_part(g, at(n, CHUNK))
                sre, sim, rre, rim = (new[c * ROWS:(c + 1) * ROWS] for c in range(4))
                src_out[0, f, :, at(n, CHUNK)] = sre.astype(BF16)
                src_out[1, f, :, at(n, CHUNK)] = sim.astype(BF16)
                rcv_out[0, f, :, at(n, CHUNK)] = rre.astype(BF16)
                rcv_out[1, f, :, at(n, CHUNK)] = rim.astype(BF16)
                image += wt[f] * (sre * rre + sim * rim)
            pair[n, core] = image.astype(BF16)
            pair_copy(n).start()
        for n in range(4):
            pass_on(n)

    arrivals(A2A4, got4, plane, ROWS, use4, last4)

    wait_on(rs.at[DIST0], dist0.at[0])
    wait_on(rs.at[DIST1], dist1.at[0])
    hands = [remote(dist0.at[core], dist0.at[core], HAND0, fq + 1 - 2 * core, s),
             remote(dist1.at[core], dist1.at[core], HAND1, fq + 1 - 2 * core, s)]
    for hand in hands:
        hand.start()
        pending.append(hand.wait_send)
    for hand in hands:
        hand.wait_recv()
    for j in range(8):
        grad[0, :, pl.ds(j * LANES, LANES)] = dist0[j % 2, j // 2].astype(F32)
        tile = dist1[0, 2 * j].astype(F32)
        block = lanes(tile) // BLOCK
        for p in range(1, 4):
            tile = jnp.where(block == p, dist1[p % 2, 2 * j + p // 2].astype(F32), tile)
        grad[1, :, pl.ds(j * LANES, LANES)] = tile

    for wait in pending:
        wait()

    for n in range(4):
        cross_copy(n).wait_recv()
        grad[2, :, at(n, CHUNK)] = cross[n, 0].astype(F32) + cross[n, 1].astype(F32)


def on_device(source_field, receiver_field, line_inverse, lens_delay, omegas, image_weights):
    vmem = pltpu.VMEM
    plane = vmem((NL, LANES), BF16)
    fields, gradient = pl.pallas_call(
        kernel,
        out_shape=(
            vmem((2,) + source_field.shape, BF16),
            vmem(lens_delay.shape, F32),
        ),
        in_specs=[pl.BlockSpec(memory_space=pl.ANY)] * 6,
        out_specs=[pl.BlockSpec(memory_space=vmem)] * 2,
        scratch_shapes=[
            vmem(source_field.shape, BF16), vmem(receiver_field.shape, BF16), vmem(lens_delay.shape, F32),
            vmem((2, 2, NL, NL), BF16), vmem((2, 2, NL, NL), BF16),
            plane, plane, plane, plane, plane, plane, plane, plane,
            plane, vmem((2, NL, LANES), BF16),
            vmem((2, LANES, NL), BF16), vmem((2, LANES, NL), BF16), vmem((2, 2, 64, NL), BF16),
            vmem((NL, LANES), F32), vmem((LANES, NL), F32), vmem((2, 64, NL), F32),
            vmem((BLOCK, NL), F32), vmem((BLOCK, NL), F32),
            vmem((NL, LANES), F32), vmem((NL, LANES), F32),
            vmem((2, ROWS, NL), F32), vmem((GROUP * ROWS, LANES), BF16), plane,
            vmem((8, BLOCK, LANES), BF16), vmem((8, BLOCK, LANES), BF16),
            vmem((BLOCK, LANES), BF16), vmem((2, 4, ROWS, LANES), BF16),
            vmem((8, BLOCK, LANES), BF16), vmem((8, BLOCK, LANES), BF16),
            vmem((4, BLOCK, LANES), BF16), vmem((2, GROUP // 2, ROWS, LANES), BF16),
            vmem((4, 2, ROWS, CHUNK), BF16), vmem((4, 2, ROWS, CHUNK), BF16),
            pltpu.SMEM((2,), F32), pltpu.SMEM((2,), F32),
            pltpu.SemaphoreType.DMA((7,)),
            pltpu.SemaphoreType.DMA((PHASES,)),
            pltpu.SemaphoreType.DMA((PHASES,)),
            pltpu.SemaphoreType.DMA((16,)),
        ],
        compiler_params=pltpu.CompilerParams(
            collective_id=0, has_side_effects=True, vmem_limit_bytes=60 * 2**20),
    )(source_field, receiver_field, line_inverse, lens_delay, omegas, image_weights)
    return fields[0], fields[1], gradient


def solution(mesh):
    placed = (
        P(None, "freq", "space", None),
        P(None, "freq", "space", None),
        P(None, "freq", None, None),
        P(None, "space", None),
        P("freq"),
        P("freq"),
    )
    return jax.shard_map(
        on_device,
        mesh=mesh,
        in_specs=placed,
        out_specs=(
            P(None, "freq", "space", None),
            P(None, "freq", "space", None),
            P(None, "space", None),
        ),
        check_vma=False,
    )
```

```python
import jax
import jax.numpy as jnp
from jax import lax
from jax.experimental import pallas as pl
from jax.experimental.pallas import tpu as pltpu
from jax.sharding import PartitionSpec as P

F32 = jnp.float32
BF16 = jnp.bfloat16
MESH = pl.DeviceIdType.MESH
LANES = 128
BLOCK = 32
NL = 1024
ROWS = 16
GROUP = 32
SHARDS = 64
CHUNK = 256
SWAP_SIGN = (-1.0, 1.0, 1.0, -1.0)

(A2A1, A2A2, A2A3, A2A4, LENS1, LENS2, FWD1, FWD2,
 SUM0, DIST0, SUM1, DIST1, PAIR, _, _, _, CROSS, _, _, _, HAND0, HAND1) = range(22)
PHASES = 22


def lanes(tile):
    return lax.broadcasted_iota(jnp.int32, tile.shape, 1)


def turn(tile, shift):
    return pltpu.roll(tile, shift % LANES, 1)


def even_block(tile):
    return (lanes(tile) // BLOCK) % 2 == 0


def block_transpose(tiles):
    t0, t1, t2, t3 = tiles
    low = lanes(t0) < 64
    even = even_block(t0)
    a0, a2 = jnp.where(low, t0, turn(t2, 64)), jnp.where(low, turn(t0, 64), t2)
    a1, a3 = jnp.where(low, t1, turn(t3, 64)), jnp.where(low, turn(t1, 64), t3)
    b0, b1 = jnp.where(even, a0, turn(a1, 32)), jnp.where(even, turn(a0, -32), a1)
    b2, b3 = jnp.where(even, a2, turn(a3, 32)), jnp.where(even, turn(a2, -32), a3)
    return b0, b1, b2, b3


def swap_parts(tile):
    return jnp.where(even_block(tile), turn(tile, -32), turn(tile, 32))


def outer_sign(tile):
    block = lanes(tile) // BLOCK
    return jnp.where((block == 0) | (block == 3), -1.0, 1.0)


def cos_sin(theta):
    n = jnp.floor(theta * 0.3183098861837907 + 0.5)
    r = theta - n * 3.140625
    r = r - n * 9.67502593994140625e-4
    r = r - n * 1.509957990978376e-7
    flip = 1.0 - 2.0 * (n - 2.0 * jnp.floor(n * 0.5))
    z = r * r
    s = -1.0 / 39916800.0
    for term in (1.0 / 362880.0, -1.0 / 5040.0, 1.0 / 120.0, -1.0 / 6.0, 1.0):
        s = s * z + term
    c = 1.0 / 479001600.0
    for term in (-1.0 / 3628800.0, 1.0 / 40320.0, -1.0 / 720.0, 1.0 / 24.0, -0.5, 1.0):
        c = c * z + term
    return c * flip, s * r * flip


def at(index, size):
    start = index * size
    return pl.ds(start if isinstance(start, int) else pl.multiple_of(start, size), size)


def kernel(src, rcv, minv, lens, om_hbm, wt_hbm, fields, grad,
           src_v, rcv_v, lens_v, m, mt, send1, got1, send2, got2, send3, got3, send4, got4,
           ya, yb, xa, xb, xf, acc_y, acc_x, acc_f, cos1, sin1, cos2, sin2, lens1, lens2_send, lens2,
           part0, sum0, dist0_send, dist0, part1, sum1, dist1_send, dist1,
           pair, cross, om, wt, load_sem, ss, rs, parts):
    src_out, rcv_out = fields.at[0], fields.at[1]
    fq = lax.axis_index("freq")
    s = lax.axis_index("space")
    h = s // GROUP
    k = lax.rem(s, GROUP)
    core = lax.rem(fq, 2)
    z_hi = fq // 2
    rank = 2 * fq + h
    mine = lax.rem(s, 2) == core

    def remote(source, target, phase, freq, space):
        return pltpu.make_async_remote_copy(
            src_ref=source, dst_ref=target, send_sem=ss.at[phase], recv_sem=rs.at[phase],
            device_id={"freq": freq, "space": space}, device_id_type=MESH)

    quarter = k // 8
    plane = s // 16

    def transposed(source, target, phase, part, space):
        pltpu.make_async_remote_copy(
            src_ref=source, dst_ref=target, send_sem=ss.at[phase], recv_sem=parts.at[4 * phase + part],
            device_id={"freq": fq, "space": space}, device_id_type=MESH).start()

    def wait_on(sem, ref):
        pltpu.make_async_copy(ref, ref, sem).wait()

    def give(source, target, phase, freq, space):
        here = (freq == fq) & (space == s)

        @pl.when(here)
        def _():
            pltpu.make_async_copy(source, target, rs.at[phase]).start()

        @pl.when(jnp.logical_not(here))
        def _():
            remote(source, target, phase, freq, space).start()

    loads = [
        pltpu.make_async_copy(src, src_v, load_sem.at[0]),
        pltpu.make_async_copy(rcv, rcv_v, load_sem.at[1]),
        pltpu.make_async_copy(lens, lens_v, load_sem.at[2]),
        pltpu.make_async_copy(om_hbm, om, load_sem.at[5]),
        pltpu.make_async_copy(wt_hbm, wt, load_sem.at[6]),
        pltpu.make_async_copy(minv.at[:, h], m.at[0], load_sem.at[3]),
        pltpu.make_async_copy(minv.at[:, 1 - h], m.at[1], load_sem.at[4]),
    ]
    for load in loads:
        load.start()
    barrier = pltpu.get_barrier_semaphore()
    pending = []
    own1 = (s == 0) | (s == SHARDS - 1)

    def sent(phase, ref, condition=None):
        def wait():
            if condition is None:
                wait_on(ss.at[phase], ref)
            else:
                pl.when(condition)(lambda: wait_on(ss.at[phase], ref))

        pending.append(wait)


    def greet(i, carry):
        pl.semaphore_signal(barrier, inc=1, device_id={"freq": fq, "space": lax.rem(s + i, SHARDS)},
                            device_id_type=MESH)
        return carry

    lax.fori_loop(1, SHARDS, greet, 0)
    for i in range(1, 4):
        pl.semaphore_signal(barrier, inc=1, device_id={"freq": lax.rem(fq + i, 4), "space": s},
                            device_id_type=MESH)
    for load in loads[:5]:
        load.wait()
    om_h = om[h]
    wt_h = wt[h]

    def rotate0(i, carry):
        f = i // 8
        q = lax.rem(i, 8)
        c, sn = cos_sin(om[f] * lens_v[0, :, at(q, LANES)])
        sre = src_v[0, f, :, at(q, LANES)].astype(F32)
        sim = src_v[1, f, :, at(q, LANES)].astype(F32)
        rre = rcv_v[0, f, :, at(q, LANES)].astype(F32)
        rim = rcv_v[1, f, :, at(q, LANES)].astype(F32)
        tiles = block_transpose((sre * c + sim * sn, sim * c - sre * sn,
                                 rre * c - rim * sn, rim * c + rre * sn))
        for p in range(4):
            send1[at(f * GROUP + 4 * q + p, ROWS), :] = tiles[p].astype(BF16)
        return carry

    lax.fori_loop(0, 16, rotate0, 0)
    got1[at(s, ROWS), :] = send1[at(s, ROWS), :]
    pl.semaphore_wait(barrier, SHARDS - 1 + 3)

    def send_all(send, got, phase, n):
        def one(i):
            t = n * 16 + lax.rem(s + i, 16)
            transposed(send.at[at(t, ROWS)], got.at[at(s, ROWS)], phase, plane, t)

        pl.when(n != plane)(lambda: one(0))
        for i in range(1, 16):
            one(i)

    def go1(i, carry):
        send_all(send1, got1, A2A1, lax.rem(plane + i, 4))
        return carry

    lax.fori_loop(0, 4, go1, 0)
    sent(A2A1, send1.at[pl.ds(0, ROWS * (SHARDS - 1))])

    @pl.when(mine)
    def _():
        for half in range(2):
            give(lens_v.at[1], lens1.at[core], LENS1, fq, half * GROUP + s // 2)

    sent(LENS1, lens_v.at[1], mine & own1)
    sent(LENS1, lens_v.at[pl.ds(0, 2)], mine & jnp.logical_not(own1))

    def pack2(q, carry):
        value = lens_v[2, :, at(q, LANES)]
        high = value.astype(BF16).astype(F32)
        rest = value - high
        middle = rest.astype(BF16).astype(F32)
        tiles = block_transpose((high, middle, rest - middle, jnp.zeros_like(value)))
        for p in range(4):
            lens2_send[at(4 * q + p, ROWS), :] = tiles[p].astype(BF16)
        return carry

    lax.fori_loop(0, 8, pack2, 0)

    def arrivals(phase, got, own, lines, use, last):
        for i in range(4):
            g = lax.rem(own + 4 - i, 4)
            wait_on(parts.at[4 * phase + g], got.at[pl.ds(0, CHUNK - (lines if i == 0 else 0))])
            if i < 3:
                use(g, i)
            else:
                last(g)

    def y_operands(got, other, g):
        for u in range(2):
            rows = at(2 * g + u, 128)
            tile = got[rows, :].astype(F32)
            other[rows, :] = (swap_parts(tile) * outer_sign(tile)).astype(BF16)

    def y_arrivals(phase, got, own, lines, start, finish):
        def part(g, rows):
            return (jnp.dot(m[0, 0, rows, at(g, CHUNK)], got[at(g, CHUNK), :], preferred_element_type=F32)
                    + jnp.dot(m[0, 1, rows, at(g, CHUNK)], ya[at(g, CHUNK), :], preferred_element_type=F32))

        def use(g, i):
            y_operands(got, ya, g)

            def body(n, carry):
                rows = at(n, CHUNK)
                acc_y[rows, :] = part(g, rows) if i == 0 else acc_y[rows, :] + part(g, rows)
                return carry

            lax.fori_loop(0, 4, body, 0)

        def last(g):
            y_operands(got, ya, g)

            def body(i, carry):
                n = lax.rem(start + i, 4)
                rows = at(n, CHUNK)
                finish(n, acc_y[rows, :] + part(g, rows))
                return carry

            lax.fori_loop(0, 4, body, 0)

        arrivals(phase, got, own, lines, use, last)

    def y_solve(first, second, n):
        rows = at(n, CHUNK)
        return (jnp.dot(m[0, 0, rows, :], first[...], preferred_element_type=F32)
                + jnp.dot(m[0, 1, rows, :], second[...], preferred_element_type=F32))

    def x_solve(f, first, second, n):
        columns = at(n, CHUNK)
        return (jnp.dot(first, mt[f, 0, :, columns], preferred_element_type=F32)
                + jnp.dot(second, mt[f, 1, :, columns], preferred_element_type=F32))

    def flip_matrix(f, begin, end):
        def body(i, carry):
            part = i // 8
            r = lax.rem(i, 8)
            mt[f, part, :, at(r, LANES)] = m[f, part, at(r, LANES), :].T
            return carry

        lax.fori_loop(begin, end, body, 0)

    def send_group(send, got, phase, n):
        def one(i):
            t = n * 8 + lax.rem(k + i, 8)
            transposed(send.at[at(t, BLOCK)], got.at[at(k, BLOCK)], phase, quarter, h * GROUP + t)

        pl.when(n != quarter)(lambda: one(0))
        for i in range(1, 8):
            one(i)

    loads[5].wait()
    flip_matrix(0, 0, 16)
    loads[6].wait()
    flip_matrix(1, 0, 16)

    def finish1(n, new):
        send2[at(n, CHUNK), :] = new.astype(BF16)
        send_group(send2, got2, A2A2, n)

    y_arrivals(A2A1, got1, plane, ROWS, quarter, finish1)
    sent(A2A2, send2.at[pl.ds(0, BLOCK * (GROUP - 1))])
    got2[at(k, BLOCK), :] = send2[at(k, BLOCK), :]

    wait_on(rs.at[LENS1], lens1.at[0])
    forward1 = remote(lens1.at[core], lens1.at[core], FWD1, fq + 1 - 2 * core, s)
    forward1.start()
    pending.append(forward1.wait_send)

    skew = jnp.where(mine, 0, 1)

    def go_lens2(i):
        t = lax.rem(s + skew + 2 * i, SHARDS)
        remote(lens2_send.at[at(lax.rem(t, GROUP), ROWS)], lens2.at[at(s, ROWS)], LENS2, fq, t).start()

    pl.when(jnp.logical_not(mine))(lambda: go_lens2(0))
    for i in range(1, 32):
        go_lens2(i)
    sent(LENS2, lens2_send.at[pl.ds(0, ROWS * 31)], mine)
    sent(LENS2, lens2_send, jnp.logical_not(mine))

    @pl.when(mine)
    def _():
        lens2[at(s, ROWS), :] = lens2_send[at(k, ROWS), :]

    forward1.wait_recv()

    def trig1(q, carry):
        for b in range(2):
            c, sn = cos_sin(om_h * lens1[b, :, at(q, LANES)])
            cos1[pl.ds(b * ROWS, ROWS), at(q, LANES)] = c
            sin1[pl.ds(b * ROWS, ROWS), at(q, LANES)] = sn
        return carry

    lax.fori_loop(0, 8, trig1, 0)

    def gather2(g):
        for u in range(2):
            q = 2 * g + u
            tiles = block_transpose([got2[at(4 * q + p, BLOCK), :].astype(F32) for p in range(4)])
            for c in range(4):
                xa[0, pl.ds(c * BLOCK, BLOCK), at(q, LANES)] = tiles[c].astype(BF16)
                xa[1, pl.ds(c * BLOCK, BLOCK), at(q, LANES)] = (SWAP_SIGN[c] * tiles[c ^ 1]).astype(BF16)

    def x_part(g, columns):
        return (jnp.dot(xa[0, :, at(g, CHUNK)], mt[0, 0, at(g, CHUNK), columns], preferred_element_type=F32)
                + jnp.dot(xa[1, :, at(g, CHUNK)], mt[0, 1, at(g, CHUNK), columns],
                          preferred_element_type=F32))

    def use2(g, i):
        gather2(g)

        def body(n, carry):
            columns = at(n, CHUNK)
            acc_x[:, columns] = x_part(g, columns) if i == 0 else acc_x[:, columns] + x_part(g, columns)
            return carry

        lax.fori_loop(0, 4, body, 0)

    def last2(g):
        gather2(g)

        def body(n, carry):
            solve2(n, acc_x[:, at(n, CHUNK)] + x_part(g, at(n, CHUNK)))
            return carry

        lax.fori_loop(0, 4, body, 0)

    def solve2(n, new):
        sre, sim, rre, rim = (new[c * BLOCK:(c + 1) * BLOCK] for c in range(4))
        image = wt_h * (sre * rre + sim * rim)
        for u in range(2):
            part0[2 * n + u] = image[:, u * LANES:(u + 1) * LANES].astype(BF16)
        c, sn = cos1[:, at(n, CHUNK)], sin1[:, at(n, CHUNK)]
        turned = (sre * c + sim * sn, sim * c - sre * sn, rre * c - rim * sn, rim * c + rre * sn)
        for part in range(4):
            xb[0, pl.ds(part * BLOCK, BLOCK), at(n, CHUNK)] = turned[part].astype(BF16)
            xb[1, pl.ds(part * BLOCK, BLOCK), at(n, CHUNK)] = (
                SWAP_SIGN[part] * turned[part ^ 1]).astype(BF16)

    arrivals(A2A2, got2, quarter, BLOCK, use2, last2)

    forward2 = remote(lens2, lens2, FWD2, fq + 1 - 2 * core, s)

    @pl.when(mine)
    def _():
        wait_on(rs.at[LENS2], lens2.at[pl.ds(0, ROWS * (SHARDS - 1))])
        forward2.start()

    def solve3(i, carry):
        n = lax.rem(k // 8 + i, 4)
        new = x_solve(0, xb[0], xb[1], n)
        for u in range(2):
            tiles = block_transpose([new[c * BLOCK:(c + 1) * BLOCK, u * LANES:(u + 1) * LANES]
                                     for c in range(4)])
            for p in range(4):
                send3[at(8 * n + 4 * u + p, BLOCK), :] = tiles[p].astype(BF16)
        send_group(send3, got3, A2A3, n)
        return carry

    lax.fori_loop(0, 4, solve3, 0)
    sent(A2A3, send3.at[pl.ds(0, BLOCK * (GROUP - 1))])
    got3[at(k, BLOCK), :] = send3[at(k, BLOCK), :]

    def sum_send(part, total, phase):
        total[rank] = part[rank]

        def body(i, carry):
            j = lax.rem(rank + i, 8)
            remote(part.at[j], total.at[rank], phase, j // 2, lax.rem(j, 2) * GROUP + k).start()
            return carry

        lax.fori_loop(1, 8, body, 0)
        sent(phase, part.at[pl.ds(0, 7)])

    def sum_up(total, phase):
        wait_on(rs.at[phase], total.at[pl.ds(0, 7)])
        value = total[0].astype(F32)
        for j in range(1, 8):
            value += total[j].astype(F32)
        return value

    sum_send(part0, sum0, SUM0)

    @pl.when(jnp.logical_not(mine))
    def _():
        forward2.wait_recv()

    sent(FWD2, lens2, mine)

    def trig2(i, carry):
        terms = lens2[at(i, 128), :].astype(F32)
        value = (terms + turn(terms, -32)) + turn(terms, -64)
        value = jnp.where(lanes(value) < BLOCK, value, 0.0)
        value = value + turn(value, 32)
        value = value + turn(value, 64)
        c, sn = cos_sin(om_h * value)
        cos2[at(i, 128), :] = c
        sin2[at(i, 128), :] = -outer_sign(sn) * sn
        return carry

    lax.fori_loop(0, 8, trig2, 0)

    def solve4(n, new):
        product = wt_h * new * turn(new, 64)
        image = product + turn(product, -32)
        for u in range(2):
            packed = image[u * 128:u * 128 + BLOCK]
            block = lanes(packed) // BLOCK
            for a in range(1, 4):
                rows = image[u * 128 + a * BLOCK:u * 128 + (a + 1) * BLOCK]
                packed = jnp.where(block == a, turn(rows, a * BLOCK), packed)
            part1[2 * n + u] = packed.astype(BF16)
        turned = new * cos2[at(n, CHUNK), :] + swap_parts(new) * sin2[at(n, CHUNK), :]
        yb[0, at(n, CHUNK), :] = turned.astype(BF16)
        yb[1, at(n, CHUNK), :] = (swap_parts(turned) * outer_sign(turned)).astype(BF16)

    y_arrivals(A2A3, got3, quarter, BLOCK, 0, solve4)
    sum_send(part1, sum1, SUM1)

    def solve5(i, carry):
        n = lax.rem(plane + i, 4)
        send4[at(n, CHUNK), :] = y_solve(yb.at[0], yb.at[1], n).astype(BF16)

        send_all(send4, got4, A2A4, n)
        return carry

    lax.fori_loop(0, 4, solve5, 0)
    sent(A2A4, send4.at[pl.ds(0, ROWS * (SHARDS - 1))])
    got4[at(s, ROWS), :] = send4[at(s, ROWS), :]

    dist0_send[...] = sum_up(sum0, SUM0).astype(BF16)
    for up in range(2):
        for b in range(2):
            give(dist0_send.at[pl.ds(b * ROWS, ROWS)], dist0.at[h, fq], DIST0, 2 * up + h, 2 * k + b)
    sent(DIST0, dist0.at[0, pl.ds(0, 3)], own1 & (core == h))
    sent(DIST0, dist0.at[0], jnp.logical_not(own1 & (core == h)))

    total1 = sum_up(sum1, SUM1)
    for d in range(4):
        dist1_send[d] = turn(total1, d * BLOCK).astype(BF16)

    side = lax.rem(k, 2)

    def dist1_copy(i):
        d = lax.rem(k + 4 - i // 2, 4)
        return dist1_send.at[d, at(i % 2, ROWS)], dist1.at[side, k // 2], DIST1

    for i in range(8):
        remote(*dist1_copy(i), side + 2 * (1 - z_hi), 8 * rank + i).start()
    for i in range(8):
        give(*dist1_copy(i), side + 2 * z_hi, 8 * rank + i)
    own_dist = (s // 8 == rank) & (core == side)
    sent(DIST1, dist1.at[0, pl.ds(0, 15)], own_dist)
    sent(DIST1, dist1.at[0], jnp.logical_not(own_dist))

    acc_f[...] = jnp.zeros_like(acc_f)

    def gather4(g):
        f = g // 2
        for u in range(4):
            q = 4 * lax.rem(g, 2) + u
            tiles = block_transpose([got4[at(f * GROUP + 4 * q + p, ROWS), :].astype(F32) for p in range(4)])
            for c in range(4):
                xf[f, 0, pl.ds(c * ROWS, ROWS), at(q, LANES)] = tiles[c].astype(BF16)
                xf[f, 1, pl.ds(c * ROWS, ROWS), at(q, LANES)] = (SWAP_SIGN[c] * tiles[c ^ 1]).astype(BF16)

    def f_part(g, columns):
        f = g // 2
        which = jnp.where(h == f, 0, 1)
        terms = at(lax.rem(g, 2), 512)
        return (jnp.dot(xf[f, 0, :, terms], mt[which, 0, terms, columns], preferred_element_type=F32)
                + jnp.dot(xf[f, 1, :, terms], mt[which, 1, terms, columns], preferred_element_type=F32))

    def use4(g, i):
        gather4(g)

        def body(n, carry):
            acc_f[g // 2, :, at(n, CHUNK)] += f_part(g, at(n, CHUNK))
            return carry

        lax.fori_loop(0, 4, body, 0)

    def pair_copy(n):
        return remote(pair.at[n, core], pair.at[n, core], PAIR + n, fq + 1 - 2 * core, s)

    def cross_copy(n):
        return remote(cross.at[n, z_hi], cross.at[n, z_hi], CROSS + n, lax.rem(fq + 2, 4), s)

    def pass_on(n):
        pair_copy(n).wait_recv()
        cross[n, z_hi] = (pair[n, 0].astype(F32) + pair[n, 1].astype(F32)).astype(BF16)
        cross_copy(n).start()
        pending.append(pair_copy(n).wait_send)
        pending.append(cross_copy(n).wait_send)

    def last4(g):
        gather4(g)
        for n in range(4):
            image = jnp.zeros((ROWS, CHUNK), F32)
            for u in range(2):
                f = g // 2 if u == 0 else 1 - g // 2
                new = acc_f[f, :, at(n, CHUNK)]
                if u == 0:
                    new += f_part(g, at(n, CHUNK))
                sre, sim, rre, rim = (new[c * ROWS:(c + 1) * ROWS] for c in range(4))
                src_out[0, f, :, at(n, CHUNK)] = sre.astype(BF16)
                src_out[1, f, :, at(n, CHUNK)] = sim.astype(BF16)
                rcv_out[0, f, :, at(n, CHUNK)] = rre.astype(BF16)
                rcv_out[1, f, :, at(n, CHUNK)] = rim.astype(BF16)
                image += wt[f] * (sre * rre + sim * rim)
            pair[n, core] = image.astype(BF16)
            pair_copy(n).start()
        for n in range(4):
            pass_on(n)

    arrivals(A2A4, got4, plane, ROWS, use4, last4)

    wait_on(rs.at[DIST0], dist0.at[0])
    wait_on(rs.at[DIST1], dist1.at[0])
    hands = [remote(dist0.at[core], dist0.at[core], HAND0, fq + 1 - 2 * core, s),
             remote(dist1.at[core], dist1.at[core], HAND1, fq + 1 - 2 * core, s)]
    for hand in hands:
        hand.start()
        pending.append(hand.wait_send)
    for hand in hands:
        hand.wait_recv()
    for j in range(8):
        grad[0, :, pl.ds(j * LANES, LANES)] = dist0[j % 2, j // 2].astype(F32)
        tile = dist1[0, 2 * j].astype(F32)
        block = lanes(tile) // BLOCK
        for p in range(1, 4):
            tile = jnp.where(block == p, dist1[p % 2, 2 * j + p // 2].astype(F32), tile)
        grad[1, :, pl.ds(j * LANES, LANES)] = tile

    for wait in pending:
        wait()

    for n in range(4):
        cross_copy(n).wait_recv()
        grad[2, :, at(n, CHUNK)] = cross[n, 0].astype(F32) + cross[n, 1].astype(F32)


def on_device(source_field, receiver_field, line_inverse, lens_delay, omegas, image_weights):
    vmem = pltpu.VMEM
    plane = vmem((NL, LANES), BF16)
    fields, gradient = pl.pallas_call(
        kernel,
        out_shape=(
            vmem((2,) + source_field.shape, BF16),
            vmem(lens_delay.shape, F32),
        ),
        in_specs=[pl.BlockSpec(memory_space=pl.ANY)] * 6,
        out_specs=[pl.BlockSpec(memory_space=vmem)] * 2,
        scratch_shapes=[
            vmem(source_field.shape, BF16), vmem(receiver_field.shape, BF16), vmem(lens_delay.shape, F32),
            vmem((2, 2, NL, NL), BF16), vmem((2, 2, NL, NL), BF16),
            plane, plane, plane, plane, plane, plane, plane, plane,
            plane, vmem((2, NL, LANES), BF16),
            vmem((2, LANES, NL), BF16), vmem((2, LANES, NL), BF16), vmem((2, 2, 64, NL), BF16),
            vmem((NL, LANES), F32), vmem((LANES, NL), F32), vmem((2, 64, NL), F32),
            vmem((BLOCK, NL), F32), vmem((BLOCK, NL), F32),
            vmem((NL, LANES), F32), vmem((NL, LANES), F32),
            vmem((2, ROWS, NL), F32), vmem((GROUP * ROWS, LANES), BF16), plane,
            vmem((8, BLOCK, LANES), BF16), vmem((8, BLOCK, LANES), BF16),
            vmem((BLOCK, LANES), BF16), vmem((2, 4, ROWS, LANES), BF16),
            vmem((8, BLOCK, LANES), BF16), vmem((8, BLOCK, LANES), BF16),
            vmem((4, BLOCK, LANES), BF16), vmem((2, GROUP // 2, ROWS, LANES), BF16),
            vmem((4, 2, ROWS, CHUNK), BF16), vmem((4, 2, ROWS, CHUNK), BF16),
            pltpu.SMEM((2,), F32), pltpu.SMEM((2,), F32),
            pltpu.SemaphoreType.DMA((7,)),
            pltpu.SemaphoreType.DMA((PHASES,)),
            pltpu.SemaphoreType.DMA((PHASES,)),
            pltpu.SemaphoreType.DMA((16,)),
        ],
        compiler_params=pltpu.CompilerParams(
            collective_id=0, has_side_effects=True, vmem_limit_bytes=60 * 2**20),
    )(source_field, receiver_field, line_inverse, lens_delay, omegas, image_weights)
    return fields[0], fields[1], gradient


def solution(mesh):
    placed = (
        P(None, "freq", "space", None),
        P(None, "freq", "space", None),
        P(None, "freq", None, None),
        P(None, "space", None),
        P("freq"),
        P("freq"),
    )
    return jax.shard_map(
        on_device,
        mesh=mesh,
        in_specs=placed,
        out_specs=(
            P(None, "freq", "space", None),
            P(None, "freq", "space", None),
            P(None, "space", None),
        ),
        check_vma=False,
    )
```
